32 devices in a mesh: track: 4 (over x, core), tile: 8 (over z, y).
Axes of the slice: x: 2, y: 2, z: 4, core: 2. Of those that a mesh axis runs over, the one named last changes fastest.
Arguments:
- panels: bfloat16 [32768, 1024], P(('track', 'tile')), may hold values from -6 to 6
- phases: float32 [2048], P(('track', 'tile')), may hold values from -3.140625 to 3.140625
- weight_tiles: bfloat16 [4, 1024, 512], replicated, may hold values from -0.015625 to 0.015625
- tile_class: int32 [128], P(('track', 'tile')), may hold values from 0 to 3
- send_slots: int32 [24576], P(('track', 'tile')), may hold values from -1 to 1023, as said below
- foot_slot: int32 [128, 512], P(('track', 'tile')), may hold values from 0 to 767, as said below
- foot_ping: int32 [128, 512], P(('track', 'tile')), may hold values from 0 to 2047, as said below
- tile_counts: int32 [128], P(('track', 'tile')), may hold values from 102 to 512, as said below
Outputs:
- image: float32 [128, 2, 1024], P(('track', 'tile'))
- ping_gradient: float32 [2048], P(('track', 'tile'))
The draws below stay inside these ranges and needn't reach their ends.
Inputs may be any that keep to these rules, and one draw needn't show every extreme that they name: `send_slots`: entries name local panel rows of the sending device; an entry is -1 exactly where the track group of its offset (offset minus 1) lies outside the slice. `foot_slot`: the entries of one tile are distinct slots, each of which holds a panel. foot_ping[t, f] is the ping of the panel in slot foot_slot[t, f] of tile t's device. `tile_counts`: only the first tile_counts_t entries of tile t's footprint lists are used.
All inputs are finite; a program needn't handle non-finite values.
Results may differ from the reference program's by a relative error of at most 0.0065.
Values may be sent and summed in bfloat16 or wider, within the bound.
A program may use at most 128 MiB of HBM per device.

```python
import jax
import jax.numpy as jnp
from jax import lax

BINS = 512
RBLK = 16
TPIX = 1024
NWT = 4
TILES_DEV = 4
FOOT = 512
BLK = 128
GROUP = 256
PING_DEV = 64
CAP = 32
PINGS = 2048
TILES = 128
N_TRACK = 4
N_TILE = 8


def routing_tables(key):
    key_send, key_rank = jax.random.split(jax.random.fold_in(key, 11))
    rows_dev = PING_DEV * RBLK
    send_shape = (N_TRACK, N_TILE, 3, N_TILE, CAP)
    sent = jax.random.randint(key_send, send_shape, 0, rows_dev, dtype=jnp.int32)
    sender_track = lax.broadcasted_iota(jnp.int32, send_shape, 0)
    send_offset = lax.broadcasted_iota(jnp.int32, send_shape, 2)
    target_track = sender_track + send_offset - 1
    sent = jnp.where((target_track >= 0) & (target_track < N_TRACK), sent, -1)
    recv_shape = (N_TRACK, N_TILE, TILES_DEV, 3, N_TILE, CAP)
    recv_track = lax.broadcasted_iota(jnp.int32, recv_shape, 0)
    recv_offset = lax.broadcasted_iota(jnp.int32, recv_shape, 3)
    recv_source = lax.broadcasted_iota(jnp.int32, recv_shape, 4)
    recv_slot = lax.broadcasted_iota(jnp.int32, recv_shape, 5)
    from_track = recv_track + recv_offset - 1
    inside = (from_track >= 0) & (from_track < N_TRACK)
    flat_pos = (recv_offset * N_TILE + recv_source) * CAP + recv_slot
    scores = jax.random.randint(key_rank, recv_shape, 0, 1 << 20, dtype=jnp.int32)
    sort_keys = jnp.where(inside, scores * (3 * GROUP) + flat_pos, (1 << 30) + flat_pos)
    sort_keys = sort_keys.reshape(N_TRACK * N_TILE * TILES_DEV, 3 * GROUP)
    ranking = jnp.argsort(sort_keys, axis=1, stable=True)[:, :FOOT].astype(jnp.int32)
    row_device = jnp.arange(N_TRACK * N_TILE * TILES_DEV, dtype=jnp.int32)[:, None] // TILES_DEV
    own_track = row_device // N_TILE
    own_tile = row_device % N_TILE
    offset = ranking // GROUP
    source_tile = ranking // CAP % N_TILE
    slot_pos = ranking % CAP
    source_track = jnp.clip(own_track + offset - 1, 0, N_TRACK - 1)
    local_row = sent[source_track, source_tile, 2 - offset, own_tile, slot_pos]
    pings = (source_track * N_TILE + source_tile) * PING_DEV + jnp.maximum(local_row, 0) // RBLK
    return (sent.reshape(-1), ranking, pings.astype(jnp.int32))


def draw_send_slots(key, part):
    return routing_tables(key)[0]


def draw_foot_slot(key, part):
    return routing_tables(key)[1]


def draw_foot_ping(key, part):
    return routing_tables(key)[2]


def draw_tile_counts(key, part):
    key_div, key_pick = jax.random.split(jax.random.fold_in(key, 5))
    total = N_TRACK * N_TILE * TILES_DEV
    divisor = jax.random.randint(key_div, (total,), 1, 6, dtype=jnp.int32)
    counts = FOOT // divisor
    chosen = jax.random.randint(key_pick, (), 0, total, dtype=jnp.int32)
    return jnp.where(jnp.arange(total, dtype=jnp.int32) == chosen, FOOT, counts).astype(jnp.int32)


def with_ends(values, own_key, least, top_value):
    dims = values.shape
    index_at = [jax.random.randint(jax.random.fold_in(own_key, axis), (), 0, dims[axis]) for axis in range(len(dims))]
    values = values.at[tuple(index_at)].set(least)
    longest = dims.index(max(dims))
    index_at[longest] = (index_at[longest] + 1) % dims[longest]
    return values.at[tuple(index_at)].set(top_value)


def level_of(rng, extent, pieces, smallest, top_value):
    factor_of = 1.0
    for dim, parts in pieces:
        heights = jax.random.uniform(jax.random.fold_in(jax.random.fold_in(rng, 6), dim), (parts,), jnp.float32, smallest / len(pieces), top_value / len(pieces))
        factor_of = factor_of * jnp.repeat(jnp.exp(heights), extent[dim] // parts).reshape((-1,) + (1,) * (len(extent) - 1 - dim))
    return factor_of


def gaussian(key, dims, spread, limit, cuts=(), kind=jnp.bfloat16):
    array = jax.random.normal(key, dims, jnp.float32) * spread
    if len(cuts) > 0:
        array = level_of(key, dims, cuts, -0.22, 0.18) * array
    return jnp.clip(array, min=-limit, max=limit).astype(kind)


def setup_inputs(seed: int = 0) -> dict:
    key_of = jax.random.split(jax.random.key(seed), 9)
    return {
        "panels": gaussian(key_of[0], (PINGS * RBLK, 2 * BINS), 1.0, 6.0, ((0, 32),)),
        "phases": jnp.clip(jax.random.uniform(key_of[1], (PINGS,), jnp.float32, -3.140625, 3.140625), -3.140625, 3.140625),
        "weight_tiles": gaussian(key_of[2], (NWT, TPIX, BINS), (BINS * FOOT // 2) ** -0.5, 0.015625),
        "tile_class": with_ends(jax.random.randint(key_of[3], (TILES,), 0, NWT), jax.random.fold_in(key_of[3], 1), 0, NWT - 1).astype(jnp.int32),
        "send_slots": draw_send_slots(jax.random.fold_in(key_of[8], 71), 0),
        "foot_slot": draw_foot_slot(jax.random.fold_in(key_of[8], 71), 0),
        "foot_ping": draw_foot_ping(jax.random.fold_in(key_of[8], 71), 0),
        "tile_counts": draw_tile_counts(jax.random.fold_in(key_of[8], 71), 0),
    }


def rotate_panels(panels, phases):
    bin_count = panels.shape[1] // 2
    blocks_per_ping = panels.shape[0] // phases.shape[0]
    cos_rows = jnp.repeat(jnp.cos(phases), blocks_per_ping)[:, None]
    sin_rows = jnp.repeat(jnp.sin(phases), blocks_per_ping)[:, None]
    real_part = panels[:, :bin_count].astype(jnp.float32)
    imag_part = panels[:, bin_count:].astype(jnp.float32)
    turned = jnp.concatenate([cos_rows * real_part - sin_rows * imag_part, sin_rows * real_part + cos_rows * imag_part], axis=1)
    return turned.astype(jnp.bfloat16)


def phase_terms(ping_ids, tile_global, ping_total, tile_total, track_groups, pixels):
    offset = (2 * ping_ids + 1) * tile_total - (2 * tile_global + 1) * ping_total
    along = offset.astype(jnp.float32) * (track_groups / (2.0 * ping_total * tile_total))
    across = (jnp.arange(pixels, dtype=jnp.int32).astype(jnp.float32) + 0.5) / pixels - 0.5
    angles = 96.0 * across[:, None] * along[None, :] + 8.0 * (along * along)[None, :]
    return jnp.cos(angles), jnp.sin(angles)


def reference(panels, phases, weight_tiles, tile_class, send_slots, foot_slot, foot_ping, tile_counts):
    rows_dev = PING_DEV * RBLK
    rotated = rotate_panels(panels, phases)
    table = send_slots.reshape(N_TRACK, N_TILE, 3, N_TILE, CAP)
    track_ids = jnp.arange(N_TRACK, dtype=jnp.int32)[:, None, None, None, None]
    tile_ids = jnp.arange(N_TILE, dtype=jnp.int32)[None, :, None, None, None]
    offsets = jnp.arange(3, dtype=jnp.int32)[None, None, :, None, None]
    source_tile = jnp.arange(N_TILE, dtype=jnp.int32)[None, None, None, :, None]
    slot_pos = jnp.arange(CAP, dtype=jnp.int32)[None, None, None, None, :]
    source_track = track_ids + offsets - 1
    inside = (source_track >= 0) & (source_track < N_TRACK)
    clipped = jnp.clip(source_track, 0, N_TRACK - 1)
    local_row = table[clipped, source_tile, 2 - offsets, tile_ids, slot_pos]
    global_row = jnp.where(inside & (local_row >= 0), (clipped * N_TILE + source_tile) * rows_dev + local_row, -1)
    global_row = global_row.reshape(N_TRACK * N_TILE, 3 * GROUP)
    owner = jnp.arange(TILES, dtype=jnp.int32) // TILES_DEV
    entry_rows = global_row[owner[:, None], foot_slot]

    def one_tile(inputs):
        tile_global, row_ids, ping_ids, entry_count, weight_class = inputs
        weight = weight_tiles[weight_class]
        present = row_ids >= 0
        data = jnp.where(present[:, None], rotated[jnp.maximum(row_ids, 0)], jnp.zeros((), jnp.bfloat16))
        block_count = (entry_count + BLK - 1) // BLK
        positions = jnp.arange(BLK, dtype=jnp.int32)

        def block_terms(block):
            start = (block * BLK).astype(jnp.int32)
            rows = lax.dynamic_slice_in_dim(data, start, BLK, 0)
            block_pings = lax.dynamic_slice_in_dim(ping_ids, start, BLK, 0)
            cos_grid, sin_grid = phase_terms(block_pings, tile_global, PINGS, TILES, N_TRACK, TPIX)
            active = (start + positions < entry_count).astype(jnp.float32)
            real_proj = jnp.dot(weight, rows[:, :BINS].T, preferred_element_type=jnp.float32)
            imag_proj = jnp.dot(weight, rows[:, BINS:].T, preferred_element_type=jnp.float32)
            return real_proj, imag_proj, cos_grid, sin_grid, active, start

        def forward_step(block, carry):
            real_sum, imag_sum = carry
            real_proj, imag_proj, cos_grid, sin_grid, active, start = block_terms(block)
            real_sum = real_sum + jnp.sum((cos_grid * real_proj - sin_grid * imag_proj) * active[None, :], axis=1)
            imag_sum = imag_sum + jnp.sum((sin_grid * real_proj + cos_grid * imag_proj) * active[None, :], axis=1)
            return real_sum, imag_sum

        zero_row = jnp.zeros((TPIX,), jnp.float32)
        real_sum, imag_sum = lax.fori_loop(0, block_count, forward_step, (zero_row, zero_row))
        intensity = real_sum * real_sum + imag_sum * imag_sum
        heavy_real = intensity * real_sum
        heavy_imag = intensity * imag_sum

        def adjoint_step(block, values):
            real_proj, imag_proj, cos_grid, sin_grid, active, start = block_terms(block)
            adj_real = (heavy_imag[:, None] * cos_grid - heavy_real[:, None] * sin_grid).astype(jnp.bfloat16)
            adj_imag = (-(heavy_imag[:, None] * sin_grid + heavy_real[:, None] * cos_grid)).astype(jnp.bfloat16)
            correlation = jnp.sum(real_proj * adj_real.astype(jnp.float32) + imag_proj * adj_imag.astype(jnp.float32), axis=0)
            return lax.dynamic_update_slice_in_dim(values, correlation * active, start, 0)

        values = lax.fori_loop(0, block_count, adjoint_step, jnp.zeros((FOOT,), jnp.float32))
        return jnp.stack([real_sum, imag_sum]), values

    tile_index = jnp.arange(TILES, dtype=jnp.int32)
    images, values = lax.map(one_tile, (tile_index, entry_rows, foot_ping, tile_counts, tile_class))
    ping_of = jnp.maximum(entry_rows, 0) // RBLK
    gradient = jax.ops.segment_sum(values.reshape(-1), ping_of.reshape(-1), num_segments=PINGS)
    return images, gradient
```

```python
import functools

import jax
import jax.numpy as jnp
from jax import lax
from jax.experimental import pallas as pl
from jax.experimental.pallas import tpu as pltpu
from jax.sharding import PartitionSpec as P

F32 = jnp.float32
BF16 = jnp.bfloat16
MESH = pl.DeviceIdType.MESH
CHUNK = 256
NT = (((1,), (1,)), ((), ()))


def sincos(x):
    q = jnp.floor(x * 0.6366197723675814 + 0.5)
    r = ((x - q * 1.5703125) - q * 4.837512969970703e-4) - q * 7.549789948768648e-8
    r2 = r * r
    s = r + r * r2 * (-1.6666654611e-1 + r2 * (8.3321608736e-3 + r2 * -1.9515295891e-4))
    c = 1.0 - 0.5 * r2 + r2 * r2 * (
        4.166664568298827e-2 + r2 * (-1.388731625493765e-3 + r2 * 2.443315711809948e-5)
    )
    n = q.astype(jnp.int32)
    odd = (n & 1) == 1
    sine = jnp.where(odd, c, s)
    cosine = jnp.where(odd, s, c)
    sine = jnp.where((n & 2) == 2, -sine, sine)
    cosine = jnp.where(((n + 1) & 2) == 2, -cosine, cosine)
    return sine, cosine


def pack(block):
    half = block.shape[2] // 2
    return jnp.concatenate([block[:, :, :half], block[:, :, half:]], axis=1).astype(BF16)


def unpack(block):
    wide = block.astype(F32)
    rows = wide.shape[1] // 2
    return jnp.concatenate([wide[:, :rows], wide[:, rows:]], axis=2)


def kernel(
    n_track, n_tile, tiles_here, ping_local, slots,
    panels, phase, weights, send_col, send_row, mask,
    image, gradient,
    rot, gath, e_r, e_i, z, om, q_coef, m_in, part_s, near_out, near_in, tile_out, tile_in, h_all,
    m_ss, m_rs, b_ss, b_rs, c_ss, c_rs, d_ss, d_rs, e_ss, e_rs,
):
    a = lax.axis_index("track")
    b = lax.axis_index("tile")
    rows_total, width = panels.shape
    bins = width // 2
    classes, pixels, _ = weights.shape
    chunks = pixels // CHUNK
    group_rows = 2 * tiles_here
    tile_rows = n_tile * group_rows
    rows_per_ping = rows_total // ping_local
    device = a * n_tile + b
    ping_total = n_track * n_tile * ping_local
    tile_total = n_track * n_tile * tiles_here
    ping_step = n_track / ping_total
    tile_step = n_track / tile_total
    centre = 0.5 * n_track
    inside = {0: a >= 1, 1: None, 2: a <= n_track - 2}

    def guarded(o, body):
        def run():
            body()
        if o == 1:
            run()
        else:
            pl.when(inside[o])(run)

    def peer(track, tile):
        return {"track": track, "tile": tile}

    barrier = pltpu.get_barrier_semaphore()
    for o in range(3):
        def greet(o=o):
            def one(d, c):
                pl.semaphore_signal(
                    barrier, inc=1, device_id=peer(a + o - 1, lax.rem(b + d, n_tile)), device_id_type=MESH
                )
                return c
            lax.fori_loop(1 if o == 1 else 0, n_tile, one, 0)
        guarded(o, greet)

    def rotate(i, c):
        rows = pl.ds(pl.multiple_of(i * 128, 128), 128)
        sine, cosine = sincos(phase[rows, :])
        real = panels[rows, :bins].astype(F32)
        imag = panels[rows, bins:].astype(F32)
        rot[rows, :bins] = (cosine * real - sine * imag).astype(BF16)
        rot[rows, bins:] = (sine * real + cosine * imag).astype(BF16)
        return c

    lax.fori_loop(0, rows_total // 128, rotate, 0)

    neighbours = (
        n_tile - 1
        + n_tile * (jnp.where(a >= 1, 1, 0) + jnp.where(a <= n_track - 2, 1, 0))
    )
    pl.semaphore_wait(barrier, neighbours)

    def mask_copy(k, s):
        return pltpu.make_async_remote_copy(
            src_ref=mask.at[k, s], dst_ref=m_in.at[2 - k, b],
            send_sem=m_ss.at[k, s], recv_sem=m_rs.at[2 - k, b],
            device_id=peer(a + k - 1, s), device_id_type=MESH,
        )

    def mask_arrival(o, s):
        return pltpu.make_async_remote_copy(
            src_ref=mask.at[2 - o, s], dst_ref=m_in.at[o, s],
            send_sem=m_ss.at[2 - o, s], recv_sem=m_rs.at[o, s],
            device_id=peer(a + o - 1, s), device_id_type=MESH,
        )

    def each_peer(o, act):
        def one(d, c):
            act(lax.rem(b + d, n_tile))
            return c
        lax.fori_loop(1 if o == 1 else 0, n_tile, one, 0)

    for k in (0, 2, 1):
        guarded(k, lambda k=k: each_peer(k, lambda s: mask_copy(k, s).start()))
    m_in[1, b] = mask[1, b]
    for o in (0, 2):
        @pl.when(jnp.logical_not(inside[o]))
        def _(o=o):
            m_in[o] = jnp.zeros((n_tile, group_rows, slots), F32)
            h_all[o] = jnp.zeros((n_tile, 16, pixels // 2), BF16)

    def ping_places(rows):
        ping = device * ping_local + rows // rows_per_ping
        return (ping.astype(F32) + 0.5) * ping_step - centre

    def project(o):
        local = send_col[o]
        chosen = (lax.broadcasted_iota(jnp.int32, (slots, rows_total), 1) == local)
        chosen = jnp.where(chosen, 1.0, 0.0).astype(BF16)
        for half in range(2):
            for start in range(0, bins, CHUNK):
                column = half * bins + start
                got = jnp.dot(chosen, rot[:, column:column + CHUNK], preferred_element_type=F32)
                gath[half * slots:(half + 1) * slots, start:start + CHUNK] = got.astype(BF16)
        place = ping_places(local)
        lane = lax.broadcasted_iota(jnp.int32, (slots, CHUNK), 1).astype(F32)
        across = (lane + 0.5) * (1.0 / pixels) - 0.5
        now_i, now_r = sincos(96.0 * across * place + 8.0 * (place * place))
        step_i, step_r = sincos((96.0 * CHUNK / pixels) * place)
        for c in range(chunks):
            e_r[c] = now_r
            e_i[c] = now_i
            if c < chunks - 1:
                now_r, now_i = now_r * step_r - now_i * step_i, now_r * step_i + now_i * step_r

        def one(kc, carry):
            k = kc // chunks
            c = kc - k * chunks
            y = lax.dot_general(
                gath[...], weights[k, pl.ds(pl.multiple_of(c * CHUNK, CHUNK), CHUNK), :], NT,
                preferred_element_type=F32,
            )
            turn_r, turn_i = e_r[c], e_i[c]
            z[o, k, c, :slots] = (turn_r * y[:slots] - turn_i * y[slots:]).astype(BF16)
            z[o, k, c, slots:] = (turn_i * y[:slots] + turn_r * y[slots:]).astype(BF16)
            return carry

        lax.fori_loop(0, classes * chunks, one, 0)

    def partial_sums(o):
        guarded(o, lambda: each_peer(o, lambda s: mask_arrival(o, s).wait_recv()))
        marks = m_in[o].reshape(tile_rows, slots)
        row = lax.broadcasted_iota(jnp.int32, (tile_rows, slots), 0)
        group = row // group_rows
        real_row = (row - group * group_rows) < tiles_here
        tile = ((a + o - 1) * n_tile + group) * tiles_here + lax.rem(row, tiles_here)
        place = (tile.astype(F32) + 0.5) * tile_step - centre
        w_i, w_r = sincos(-16.0 * place * ping_places(send_row[o]))
        q_coef[o, :, :slots] = jnp.where(real_row, -w_i, w_r)
        q_coef[o, :, slots:] = jnp.where(real_row, -w_r, -w_i)
        coef = jnp.concatenate(
            [jnp.where(real_row, w_r, w_i), jnp.where(real_row, -w_i, w_r)], axis=1
        )
        marks = jnp.concatenate([marks, marks], axis=1)
        for k in range(classes):
            value = jnp.where(marks == k + 1.0, coef, 0.0)
            high = value.astype(BF16)
            om[k, :tile_rows] = high
            om[k, tile_rows:] = (value - high.astype(F32)).astype(BF16)
        for c in range(chunks):
            total = jnp.dot(om[0], z[o, 0, c], preferred_element_type=F32)
            for k in range(1, classes):
                total += jnp.dot(om[k], z[o, k, c], preferred_element_type=F32)
            total = total[:tile_rows] + total[tile_rows:]
            part_s[:, :, c * CHUNK:(c + 1) * CHUNK] = total.reshape(n_tile, group_rows, CHUNK)

    def near_copy(j):
        return pltpu.make_async_remote_copy(
            src_ref=near_out.at[j], dst_ref=near_in.at[j],
            send_sem=b_ss.at[j], recv_sem=b_rs.at[j],
            device_id=peer(a + 2 * j - 1, b), device_id_type=MESH,
        )

    for o in (0, 2):
        project(o)
        partial_sums(o)
        near_out[o // 2] = pack(part_s[...])
        guarded(o, lambda o=o: near_copy(o // 2).start())
    project(1)
    partial_sums(1)

    for j in range(2):
        def add(j=j):
            near_copy(j).wait_recv()
            part_s[...] += unpack(near_in[j])
        guarded(2 - 2 * j, add)
    tile_out[...] = pack(part_s[...])
    tile_in[b] = jnp.zeros((16, pixels // 2), BF16)

    def tile_copy(s, slot):
        return pltpu.make_async_remote_copy(
            src_ref=tile_out.at[s], dst_ref=tile_in.at[slot],
            send_sem=c_ss.at[s], recv_sem=c_rs.at[slot],
            device_id=peer(a, s), device_id_type=MESH,
        )

    each_peer(1, lambda s: tile_copy(s, b).start())
    each_peer(1, lambda s: tile_copy(s, s).wait_recv())
    arrived = unpack(tile_in[...])
    own = part_s[b]
    for s in range(n_tile):
        own = own + arrived[s]
    s_r, s_i = own[:tiles_here], own[tiles_here:]
    power = s_r * s_r + s_i * s_i
    heavy = jnp.concatenate([power * s_r, power * s_i], axis=0)
    h_all[1, b] = pack(heavy[None])[0]

    def h_copy(s, slot):
        return pltpu.make_async_remote_copy(
            src_ref=h_all.at[1, b], dst_ref=h_all.at[1, slot],
            send_sem=d_ss.at[s], recv_sem=d_rs.at[slot],
            device_id=peer(a, s), device_id_type=MESH,
        )

    def h_forward(o, s):
        return pltpu.make_async_remote_copy(
            src_ref=h_all.at[1, s], dst_ref=h_all.at[2 - o, s],
            send_sem=e_ss.at[o // 2, s], recv_sem=e_rs.at[o // 2, s],
            device_id=peer(a + o - 1, b), device_id_type=MESH,
        )

    each_peer(1, lambda s: h_copy(s, b).start())
    for o in (0, 2):
        guarded(o, lambda o=o: h_forward(o, b).start())

    tile_ids = device * tiles_here + lax.broadcasted_iota(jnp.int32, (tiles_here, pixels), 0)
    at = (tile_ids.astype(F32) + 0.5) * tile_step - centre
    lane = lax.broadcasted_iota(jnp.int32, (tiles_here, pixels), 1).astype(F32)
    across = (lane + 0.5) * (1.0 / pixels) - 0.5
    t_i, t_r = sincos(8.0 * (at * at) - 96.0 * across * at)
    out_r = t_r * s_r - t_i * s_i
    out_i = t_i * s_r + t_r * s_i
    for t in range(tiles_here):
        image[t, 0:1, :] = out_r[t:t + 1]
        image[t, 1:2, :] = out_i[t:t + 1]

    def relay(s):
        h_copy(s, s).wait_recv()
        for o in (0, 2):
            guarded(o, lambda o=o: h_forward(o, s).start())

    each_peer(1, relay)

    def pull(o):
        heavy = unpack(h_all[o]).reshape(tile_rows, pixels).astype(BF16)
        marks = m_in[o].reshape(tile_rows, slots)
        marks = jnp.concatenate([marks, marks], axis=1)
        total = jnp.zeros((tile_rows, 2 * slots), F32)
        for k in range(classes):
            got = lax.dot_general(heavy[:, :CHUNK], z[o, k, 0], NT, preferred_element_type=F32)
            for c in range(1, chunks):
                got += lax.dot_general(
                    heavy[:, c * CHUNK:(c + 1) * CHUNK], z[o, k, c], NT, preferred_element_type=F32
                )
            total = jnp.where(marks == k + 1.0, got, total)
        corr = jnp.sum(total * q_coef[o], axis=0, keepdims=True)
        corr = corr[:, :slots] + corr[:, slots:]
        ping = lax.broadcasted_iota(jnp.int32, (ping_local, slots), 0)
        return jnp.where(send_row[o] // rows_per_ping == ping, corr, 0.0)

    spread = pull(1)
    for o in (0, 2):
        guarded(o, lambda o=o: lax.fori_loop(
            0, n_tile, lambda s, c: (h_forward(2 - o, s).wait_recv(), c)[1], 0))
        spread = spread + pull(o)
    gradient[...] = jnp.sum(spread, axis=1, keepdims=True)

    for k in range(3):
        guarded(k, lambda k=k: each_peer(k, lambda s: mask_copy(k, s).wait_send()))
    for o in (0, 2):
        def finish(o=o):
            near_copy(o // 2).wait_send()
            lax.fori_loop(0, n_tile, lambda s, c: (h_forward(o, s).wait_send(), c)[1], 0)
        guarded(o, finish)
    each_peer(1, lambda s: tile_copy(s, b).wait_send())
    each_peer(1, lambda s: h_copy(s, b).wait_send())


def on_device(
    panels, phases, weight_tiles, tile_class, send_slots, foot_slot, foot_ping, tile_counts
):
    n_track = lax.axis_size("track")
    n_tile = lax.axis_size("tile")
    b = lax.axis_index("tile")
    ping_local = phases.shape[0]
    rows_total, width = panels.shape
    bins = width // 2
    tiles_here, foot = foot_slot.shape
    classes, pixels, _ = weight_tiles.shape
    slots = send_slots.shape[0] // 3
    cap = slots // n_tile
    group_rows = 2 * tiles_here
    tile_rows = n_tile * group_rows
    chunks = pixels // CHUNK

    used = jnp.arange(foot, dtype=jnp.int32)[None, :] < tile_counts[:, None]
    entries = jnp.where(used, foot_slot, -1)
    hit = entries[:, :, None] == jnp.arange(3 * slots, dtype=jnp.int32)[None, None, :]
    mark = jnp.where(hit.any(axis=1), (tile_class[:, None] + 1).astype(F32), 0.0)
    mark = mark.reshape(tiles_here, 3, n_tile, cap).transpose(1, 2, 0, 3)
    mark = jnp.tile(mark, (1, 1, 2, n_tile))
    mark = jnp.where(jnp.arange(slots) // cap == b, mark, 0.0)

    phase = jnp.repeat(phases, rows_total // ping_local)[:, None]
    vmem = pl.BlockSpec(memory_space=pltpu.VMEM)
    dma = pltpu.SemaphoreType.DMA
    image, gradient = pl.pallas_call(
        functools.partial(kernel, n_track, n_tile, tiles_here, ping_local, slots),
        out_shape=(
            jax.ShapeDtypeStruct((tiles_here, 2, pixels), F32),
            jax.ShapeDtypeStruct((ping_local, 1), F32),
        ),
        in_specs=[vmem] * 6,
        out_specs=(vmem, vmem),
        scratch_shapes=[
            pltpu.VMEM((rows_total, width), BF16),
            pltpu.VMEM((2 * slots, bins), BF16),
            pltpu.VMEM((chunks, slots, CHUNK), F32),
            pltpu.VMEM((chunks, slots, CHUNK), F32),
            pltpu.VMEM((3, classes, chunks, 2 * slots, CHUNK), BF16),
            pltpu.VMEM((classes, 2 * tile_rows, 2 * slots), BF16),
            pltpu.VMEM((3, tile_rows, 2 * slots), F32),
            pltpu.VMEM((3, n_tile, group_rows, slots), F32),
            pltpu.VMEM((n_tile, group_rows, pixels), F32),
            pltpu.VMEM((2, n_tile, 2 * group_rows, pixels // 2), BF16),
            pltpu.VMEM((2, n_tile, 2 * group_rows, pixels // 2), BF16),
            pltpu.VMEM((n_tile, 2 * group_rows, pixels // 2), BF16),
            pltpu.VMEM((n_tile, 2 * group_rows, pixels // 2), BF16),
            pltpu.VMEM((3, n_tile, 2 * group_rows, pixels // 2), BF16),
            dma((3, n_tile)), dma((3, n_tile)),
            dma((2,)), dma((2,)),
            dma((n_tile,)), dma((n_tile,)),
            dma((n_tile,)), dma((n_tile,)),
            dma((2, n_tile)), dma((2, n_tile)),
        ],
        compiler_params=pltpu.CompilerParams(
            collective_id=0, has_side_effects=True, vmem_limit_bytes=52 * 1024 * 1024
        ),
    )(
        panels, phase, weight_tiles,
        send_slots.reshape(3, slots, 1), send_slots.reshape(3, 1, slots), mark,
    )
    return image, gradient.reshape(ping_local)


def solution(mesh):
    in_specs = (
        P(("track", "tile"), None),
        P(("track", "tile")),
        P(),
        P(("track", "tile")),
        P(("track", "tile")),
        P(("track", "tile"), None),
        P(("track", "tile"), None),
        P(("track", "tile")),
    )
    out_specs = (P(("track", "tile"), None, None), P(("track", "tile")))
    return jax.shard_map(
        on_device, mesh=mesh, in_specs=in_specs, out_specs=out_specs, check_vma=False
    )
```

```python
import functools

import jax
import jax.numpy as jnp
from jax import lax
from jax.experimental import pallas as pl
from jax.experimental.pallas import tpu as pltpu
from jax.sharding import PartitionSpec as P

F32 = jnp.float32
BF16 = jnp.bfloat16
MESH = pl.DeviceIdType.MESH
CHUNK = 256
NT = (((1,), (1,)), ((), ()))


def sincos(x):
    q = jnp.floor(x * 0.6366197723675814 + 0.5)
    r = ((x - q * 1.5703125) - q * 4.837512969970703e-4) - q * 7.549789948768648e-8
    r2 = r * r
    s = r + r * r2 * (-1.6666654611e-1 + r2 * (8.3321608736e-3 + r2 * -1.9515295891e-4))
    c = 1.0 - 0.5 * r2 + r2 * r2 * (
        4.166664568298827e-2 + r2 * (-1.388731625493765e-3 + r2 * 2.443315711809948e-5)
    )
    n = q.astype(jnp.int32)
    odd = (n & 1) == 1
    sine = jnp.where(odd, c, s)
    cosine = jnp.where(odd, s, c)
    sine = jnp.where((n & 2) == 2, -sine, sine)
    cosine = jnp.where(((n + 1) & 2) == 2, -cosine, cosine)
    return sine, cosine


def pack(block):
    half = block.shape[2] // 2
    return jnp.concatenate([block[:, :, :half], block[:, :, half:]], axis=1).astype(BF16)


def unpack(block):
    wide = block.astype(F32)
    rows = wide.shape[1] // 2
    return jnp.concatenate([wide[:, :rows], wide[:, rows:]], axis=2)


def kernel(
    n_track, n_tile, tiles_here, ping_local, slots,
    classes_in, counts_in, panels_hbm, phases, weights_hbm, send_row, foot,
    image, gradient,
    panels, weights, column, gath, e_r, e_i, step_r, step_i, z, om, q_coef, q_sum, mark_out, m_in, marks,
    part, near_out, near_in, tile_out, tile_in, h_all,
    l_s, m_ss, m_rs, b_ss, b_rs, c_ss, c_rs, d_ss, d_rs, e_ss, e_rs,
):
    a = lax.axis_index("track")
    b = lax.axis_index("tile")
    rows_total, width = panels.shape
    bins = width // 2
    classes, pixels, _ = weights.shape
    chunks = pixels // CHUNK
    half = CHUNK // 2
    cap = slots // n_tile
    group_rows = 2 * tiles_here
    tile_rows = n_tile * group_rows
    rows_per_ping = rows_total // ping_local
    device = a * n_tile + b
    ping_total = n_track * n_tile * ping_local
    tile_total = n_track * n_tile * tiles_here
    ping_step = n_track / ping_total
    tile_step = n_track / tile_total
    centre = 0.5 * n_track
    inside = {0: a >= 1, 2: a <= n_track - 2}

    def guarded(o, body):
        def run():
            body()
        if o == 1:
            run()
        else:
            pl.when(inside[o])(run)

    def peer(track, tile):
        return {"track": track, "tile": tile}

    def each_peer(o, act):
        def one(d, c):
            act(lax.rem(b + d, n_tile))
            return c
        lax.fori_loop(1 if o == 1 else 0, n_tile, one, 0)

    panel_load = pltpu.make_async_copy(panels_hbm, panels, l_s.at[0])
    weight_load = pltpu.make_async_copy(weights_hbm, weights, l_s.at[1])
    panel_load.start()
    weight_load.start()

    barrier = pltpu.get_barrier_semaphore()
    for o in range(3):
        guarded(o, lambda o=o: each_peer(o, lambda s: pl.semaphore_signal(
            barrier, inc=1, device_id=peer(a + o - 1, s), device_id_type=MESH)))

    entry = lax.broadcasted_iota(jnp.int32, (1, foot.shape[1]), 1)
    used = []
    for t in range(tiles_here):
        used.append(jnp.where(entry < counts_in[t], foot[t:t + 1, :], -1))
    used = jnp.concatenate(used + used, axis=0).astype(F32)
    used = used.T
    slot_lane = lax.broadcasted_iota(jnp.int32, (foot.shape[1], 3 * slots), 1).astype(F32)
    for t in range(tiles_here):
        hit = jnp.where(used[:, t:t + 1] == slot_lane, 1.0, 0.0)
        hit = jnp.max(hit, axis=0, keepdims=True) * (classes_in[t] + 1).astype(F32)
        for k in range(3):
            mark_out[k, t:t + 1, :] = hit[:, k * slots:(k + 1) * slots]
            mark_out[k, tiles_here + t:tiles_here + t + 1, :] = hit[:, k * slots:(k + 1) * slots]

    neighbours = (
        n_tile - 1
        + n_tile * (jnp.where(a >= 1, 1, 0) + jnp.where(a <= n_track - 2, 1, 0))
    )
    pl.semaphore_wait(barrier, neighbours)

    def mark_copy(k, s, slot):
        return pltpu.make_async_remote_copy(
            src_ref=mark_out.at[k], dst_ref=m_in.at[2 - k, slot],
            send_sem=m_ss.at[k, s], recv_sem=m_rs.at[2 - k, slot],
            device_id=peer(a + k - 1, s), device_id_type=MESH,
        )

    for k in (0, 2, 1):
        guarded(k, lambda k=k: each_peer(k, lambda s: mark_copy(k, s, b).start()))
    m_in[1, b] = mark_out[1]
    for c in range(chunks):
        tile_in[c, b] = jnp.zeros((2 * group_rows, half), BF16)
    for o in (0, 2):
        @pl.when(jnp.logical_not(inside[o]))
        def _(o=o):
            m_in[o] = jnp.zeros((n_tile, group_rows, slots), F32)
            for c in range(chunks):
                h_all[c, o] = jnp.zeros((n_tile, 2 * group_rows, half), BF16)

    def ping_places(rows):
        ping = device * ping_local + rows // rows_per_ping
        return (ping.astype(F32) + 0.5) * ping_step - centre

    lines = jnp.broadcast_to(send_row[...].astype(F32), (8, 3 * slots))
    column[...] = lines.T[:, :1].astype(jnp.int32)
    panel_load.wait()

    def gather(o, carry):
        local = column[pl.ds(pl.multiple_of(o * slots, slots), slots), :]
        chosen = lax.broadcasted_iota(jnp.int32, (slots, rows_total), 1) == local
        chosen = jnp.where(chosen, 1.0, 0.0).astype(BF16)
        ping = lax.broadcasted_iota(jnp.int32, (slots, ping_local), 1)
        angle = jnp.where(ping == local // rows_per_ping, phases[...], 0.0)
        sine, cosine = sincos(jnp.sum(angle, axis=1, keepdims=True))
        for start in range(0, bins, CHUNK):
            real = jnp.dot(chosen, panels[:, start:start + CHUNK], preferred_element_type=F32)
            imag = jnp.dot(
                chosen, panels[:, bins + start:bins + start + CHUNK], preferred_element_type=F32
            )
            gath[o, :slots, start:start + CHUNK] = (cosine * real - sine * imag).astype(BF16)
            gath[o, slots:, start:start + CHUNK] = (sine * real + cosine * imag).astype(BF16)
        place = ping_places(local)
        lane = lax.broadcasted_iota(jnp.int32, (slots, CHUNK), 1).astype(F32)
        across = (lane + 0.5) * (1.0 / pixels) - 0.5
        first_i, first_r = sincos(96.0 * across * place + 8.0 * (place * place))
        e_r[o] = first_r
        e_i[o] = first_i
        turn_i, turn_r = sincos((96.0 * CHUNK / pixels) * place)
        step_r[o] = jnp.broadcast_to(turn_r, (slots, CHUNK))
        step_i[o] = jnp.broadcast_to(turn_i, (slots, CHUNK))
        return carry

    lax.fori_loop(0, 3, gather, 0)

    for o in range(3):
        guarded(o, lambda o=o: each_peer(o, lambda s: mark_copy(2 - o, s, s).wait_recv()))
    lane = lax.broadcasted_iota(jnp.int32, (group_rows, slots), 1)
    for o in range(3):
        for s in range(n_tile):
            shifted = pltpu.roll(m_in[o, s], lax.rem(s - b + n_tile, n_tile) * cap, 1)
            keep = (lane >= s * cap) & (lane < (s + 1) * cap)
            marks[o, s * group_rows:(s + 1) * group_rows, :slots] = jnp.where(keep, shifted, 0.0)
        mark = marks[o, :, :slots]
        marks[o, :, slots:] = mark
        row = lax.broadcasted_iota(jnp.int32, (tile_rows, slots), 0)
        group = row // group_rows
        real_row = (row - group * group_rows) < tiles_here
        tile = ((a + o - 1) * n_tile + group) * tiles_here + lax.rem(row, tiles_here)
        place = (tile.astype(F32) + 0.5) * tile_step - centre
        line = send_row[:, o * slots:(o + 1) * slots]
        w_i, w_r = sincos(-16.0 * place * ping_places(line))
        q_coef[o, :, :slots] = jnp.where(real_row, -w_i, w_r)
        q_coef[o, :, slots:] = jnp.where(real_row, -w_r, -w_i)
        coef = jnp.concatenate(
            [jnp.where(real_row, w_r, w_i), jnp.where(real_row, -w_i, w_r)], axis=1
        )
        mark = jnp.concatenate([mark, mark], axis=1)
        for k in range(classes):
            value = jnp.where(mark == k + 1.0, coef, 0.0)
            high = value.astype(BF16)
            om[o, k, :tile_rows] = high
            om[o, k, tile_rows:] = (value - high.astype(F32)).astype(BF16)
    q_sum[...] = jnp.zeros_like(q_sum)
    weight_load.wait()

    def near_copy(c, j):
        return pltpu.make_async_remote_copy(
            src_ref=near_out.at[c, j], dst_ref=near_in.at[c, j],
            send_sem=b_ss.at[c, j], recv_sem=b_rs.at[c, j],
            device_id=peer(a + 2 * j - 1, b), device_id_type=MESH,
        )

    def tile_copy(c, s, slot):
        return pltpu.make_async_remote_copy(
            src_ref=tile_out.at[c, s], dst_ref=tile_in.at[c, slot],
            send_sem=c_ss.at[c, s], recv_sem=c_rs.at[c, slot],
            device_id=peer(a, s), device_id_type=MESH,
        )

    def h_copy(c, s, slot):
        return pltpu.make_async_remote_copy(
            src_ref=h_all.at[c, 1, b], dst_ref=h_all.at[c, 1, slot],
            send_sem=d_ss.at[c, s], recv_sem=d_rs.at[c, slot],
            device_id=peer(a, s), device_id_type=MESH,
        )

    def h_forward(c, o, s):
        return pltpu.make_async_remote_copy(
            src_ref=h_all.at[c, 1, s], dst_ref=h_all.at[c, 2 - o, s],
            send_sem=e_ss.at[c, o // 2, s], recv_sem=e_rs.at[c, o // 2, s],
            device_id=peer(a + o - 1, b), device_id_type=MESH,
        )

    def project(c):
        totals = [None, None, None]
        for k in range(classes):
            weight = weights[k, pl.ds(pl.multiple_of(c * CHUNK, CHUNK), CHUNK), :]
            for o in (0, 2, 1):
                y = lax.dot_general(gath[o], weight, NT, preferred_element_type=F32)
                turn_r, turn_i = e_r[o], e_i[o]
                z[c, k, o, :slots] = (turn_r * y[:slots] - turn_i * y[slots:]).astype(BF16)
                z[c, k, o, slots:] = (turn_i * y[:slots] + turn_r * y[slots:]).astype(BF16)
                got = jnp.dot(om[o, k], z[c, k, o], preferred_element_type=F32)
                totals[o] = got if k == 0 else totals[o] + got
        for o in range(3):
            total = (totals[o][:tile_rows] + totals[o][tile_rows:]).reshape(n_tile, group_rows, CHUNK)
            if o == 1:
                part[c] = total
            else:
                near_out[c, o // 2] = pack(total)
        for o in (0, 2):
            guarded(o, lambda o=o: near_copy(c, o // 2).start())
        for o in range(3):
            now_r, now_i, by_r, by_i = e_r[o], e_i[o], step_r[o], step_i[o]
            e_r[o] = now_r * by_r - now_i * by_i
            e_i[o] = now_r * by_i + now_i * by_r

    def reduce_tracks(c):
        for j in range(2):
            def add(j=j):
                near_copy(c, j).wait_recv()
                part[c] += unpack(near_in[c, j])
            guarded(2 - 2 * j, add)
        tile_out[c] = pack(part[c])
        each_peer(1, lambda s: tile_copy(c, s, b).start())

    def reduce_tiles(c):
        each_peer(1, lambda s: tile_copy(c, s, s).wait_recv())
        arrived = unpack(tile_in[c])
        own = part[c, b]
        for s in range(n_tile):
            own = own + arrived[s]
        s_r, s_i = own[:tiles_here], own[tiles_here:]
        power = s_r * s_r + s_i * s_i
        heavy = jnp.concatenate([power * s_r, power * s_i], axis=0)
        h_all[c, 1, b] = pack(heavy[None])[0]
        each_peer(1, lambda s: h_copy(c, s, b).start())
        for o in (0, 2):
            guarded(o, lambda o=o: h_forward(c, o, b).start())
        tile_ids = device * tiles_here + lax.broadcasted_iota(jnp.int32, (tiles_here, CHUNK), 0)
        at = (tile_ids.astype(F32) + 0.5) * tile_step - centre
        pixel = c * CHUNK + lax.broadcasted_iota(jnp.int32, (tiles_here, CHUNK), 1)
        across = (pixel.astype(F32) + 0.5) * (1.0 / pixels) - 0.5
        t_i, t_r = sincos(8.0 * (at * at) - 96.0 * across * at)
        out_r = t_r * s_r - t_i * s_i
        out_i = t_i * s_r + t_r * s_i
        here = pl.ds(pl.multiple_of(c * CHUNK, CHUNK), CHUNK)
        for t in range(tiles_here):
            image[t, 0:1, here] = out_r[t:t + 1]
            image[t, 1:2, here] = out_i[t:t + 1]

    def relay(c):
        def one(s):
            h_copy(c, s, s).wait_recv()
            for o in (0, 2):
                guarded(o, lambda o=o: h_forward(c, o, s).start())
        each_peer(1, one)

    def pull(c):
        for o in (1, 0, 2):
            if o != 1:
                guarded(o, lambda o=o: lax.fori_loop(
                    0, n_tile, lambda s, x: (h_forward(c, 2 - o, s).wait_recv(), x)[1], 0))
            heavy = unpack(h_all[c, o]).reshape(tile_rows, CHUNK).astype(BF16)
            mark = marks[o]
            total = jnp.zeros((tile_rows, 2 * slots), F32)
            for k in range(classes):
                got = lax.dot_general(heavy, z[c, k, o], NT, preferred_element_type=F32)
                total = jnp.where(mark == k + 1.0, got, total)
            q_sum[o] += total

    def stage(i, carry):
        for lag, act in enumerate((project, reduce_tracks, reduce_tiles, relay, pull)):
            @pl.when((i >= lag) & (i < chunks + lag))
            def _(lag=lag, act=act):
                act(i - lag)
        return carry

    lax.fori_loop(0, chunks + 4, stage, 0)

    ping = lax.broadcasted_iota(jnp.int32, (ping_local, slots), 0)
    spread = jnp.zeros((ping_local, slots), F32)
    for o in range(3):
        corr = jnp.sum(q_sum[o] * q_coef[o], axis=0, keepdims=True)
        corr = corr[:, :slots] + corr[:, slots:]
        line = send_row[:, o * slots:(o + 1) * slots]
        spread = spread + jnp.where(line // rows_per_ping == ping, corr, 0.0)
    sums = jnp.sum(spread, axis=1, keepdims=True)
    gradient[...] = jnp.broadcast_to(sums, (ping_local, 128)).T[:1]

    for k in range(3):
        guarded(k, lambda k=k: each_peer(k, lambda s: mark_copy(k, s, b).wait_send()))

    def finish(c, carry):
        for o in (0, 2):
            def sent(o=o):
                near_copy(c, o // 2).wait_send()
                lax.fori_loop(0, n_tile, lambda s, x: (h_forward(c, o, s).wait_send(), x)[1], 0)
            guarded(o, sent)
        each_peer(1, lambda s: tile_copy(c, s, b).wait_send())
        each_peer(1, lambda s: h_copy(c, s, b).wait_send())
        return carry

    lax.fori_loop(0, chunks, finish, 0)


def on_device(
    panels, phases, weight_tiles, tile_class, send_slots, foot_slot, foot_ping, tile_counts
):
    n_track = lax.axis_size("track")
    n_tile = lax.axis_size("tile")
    ping_local = phases.shape[0]
    rows_total, width = panels.shape
    bins = width // 2
    tiles_here, foot = foot_slot.shape
    classes, pixels, _ = weight_tiles.shape
    slots = send_slots.shape[0] // 3
    group_rows = 2 * tiles_here
    tile_rows = n_tile * group_rows
    chunks = pixels // CHUNK
    packed = (n_tile, 2 * group_rows, CHUNK // 2)
    vmem = pl.BlockSpec(memory_space=pltpu.VMEM)
    smem = pl.BlockSpec(memory_space=pltpu.SMEM)
    hbm = pl.BlockSpec(memory_space=pl.ANY)
    dma = pltpu.SemaphoreType.DMA
    image, gradient = pl.pallas_call(
        functools.partial(kernel, n_track, n_tile, tiles_here, ping_local, slots),
        out_shape=(
            jax.ShapeDtypeStruct((tiles_here, 2, pixels), F32),
            jax.ShapeDtypeStruct((1, ping_local), F32),
        ),
        in_specs=[smem, smem, hbm, vmem, hbm, vmem, vmem],
        out_specs=(vmem, vmem),
        scratch_shapes=[
            pltpu.VMEM((rows_total, width), BF16),
            pltpu.VMEM((classes, pixels, bins), BF16),
            pltpu.VMEM((3 * slots, 1), jnp.int32),
            pltpu.VMEM((3, 2 * slots, bins), BF16),
            pltpu.VMEM((3, slots, CHUNK), F32),
            pltpu.VMEM((3, slots, CHUNK), F32),
            pltpu.VMEM((3, slots, CHUNK), F32),
            pltpu.VMEM((3, slots, CHUNK), F32),
            pltpu.VMEM((chunks, classes, 3, 2 * slots, CHUNK), BF16),
            pltpu.VMEM((3, classes, 2 * tile_rows, 2 * slots), BF16),
            pltpu.VMEM((3, tile_rows, 2 * slots), F32),
            pltpu.VMEM((3, tile_rows, 2 * slots), F32),
            pltpu.VMEM((3, group_rows, slots), F32),
            pltpu.VMEM((3, n_tile, group_rows, slots), F32),
            pltpu.VMEM((3, tile_rows, 2 * slots), F32),
            pltpu.VMEM((chunks, n_tile, group_rows, CHUNK), F32),
            pltpu.VMEM((chunks, 2) + packed, BF16),
            pltpu.VMEM((chunks, 2) + packed, BF16),
            pltpu.VMEM((chunks,) + packed, BF16),
            pltpu.VMEM((chunks,) + packed, BF16),
            pltpu.VMEM((chunks, 3) + packed, BF16),
            dma((2,)),
            dma((3, n_tile)), dma((3, n_tile)),
            dma((chunks, 2)), dma((chunks, 2)),
            dma((chunks, n_tile)), dma((chunks, n_tile)),
            dma((chunks, n_tile)), dma((chunks, n_tile)),
            dma((chunks, 2, n_tile)), dma((chunks, 2, n_tile)),
        ],
        compiler_params=pltpu.CompilerParams(
            collective_id=0, has_side_effects=True, vmem_limit_bytes=52 * 1024 * 1024
        ),
    )(
        tile_class, tile_counts, panels, phases.reshape(1, ping_local), weight_tiles,
        send_slots.reshape(1, 3 * slots), foot_slot,
    )
    return image, gradient.reshape(ping_local)


def solution(mesh):
    in_specs = (
        P(("track", "tile"), None),
        P(("track", "tile")),
        P(),
        P(("track", "tile")),
        P(("track", "tile")),
        P(("track", "tile"), None),
        P(("track", "tile"), None),
        P(("track", "tile")),
    )
    out_specs = (P(("track", "tile"), None, None), P(("track", "tile")))
    return jax.shard_map(
        on_device, mesh=mesh, in_specs=in_specs, out_specs=out_specs, check_vma=False
    )
```

```python
import functools

import jax
import jax.numpy as jnp
from jax import lax
from jax.experimental import pallas as pl
from jax.experimental.pallas import tpu as pltpu
from jax.sharding import PartitionSpec as P

F32 = jnp.float32
BF16 = jnp.bfloat16
MESH = pl.DeviceIdType.MESH
CHUNK = 256
NT = (((1,), (1,)), ((), ()))


def sincos(x):
    q = jnp.floor(x * 0.6366197723675814 + 0.5)
    r = ((x - q * 1.5703125) - q * 4.837512969970703e-4) - q * 7.549789948768648e-8
    r2 = r * r
    s = r + r * r2 * (-1.6666654611e-1 + r2 * (8.3321608736e-3 + r2 * -1.9515295891e-4))
    c = 1.0 - 0.5 * r2 + r2 * r2 * (
        4.166664568298827e-2 + r2 * (-1.388731625493765e-3 + r2 * 2.443315711809948e-5)
    )
    n = q.astype(jnp.int32)
    odd = (n & 1) == 1
    sine = jnp.where(odd, c, s)
    cosine = jnp.where(odd, s, c)
    sine = jnp.where((n & 2) == 2, -sine, sine)
    cosine = jnp.where(((n + 1) & 2) == 2, -cosine, cosine)
    return sine, cosine


def pack(block):
    half = block.shape[2] // 2
    return jnp.concatenate([block[:, :, :half], block[:, :, half:]], axis=1).astype(BF16)


def unpack(block):
    wide = block.astype(F32)
    rows = wide.shape[1] // 2
    return jnp.concatenate([wide[:, :rows], wide[:, rows:]], axis=2)


def kernel(
    n_track, n_tile, tiles_here, ping_local, slots,
    classes_hbm, counts_hbm, panels_hbm, phases_hbm, weights_hbm, send_hbm, foot_hbm,
    image, gradient,
    classes_in, counts_in, panels, phases, weights, send, foot,
    column, gath, e_r, e_i, step_r, step_i, z, om, coef_t, mark_t, q_sum, mark_out, m_in,
    part, s_out, s_in, h_all,
    l_s, m_ss, m_rs, s_ss, s_rs, h_ss, h_rs,
):
    a = lax.axis_index("track")
    b = lax.axis_index("tile")
    rows_total, width = panels.shape
    bins = width // 2
    classes, pixels, _ = weights.shape
    chunks = pixels // CHUNK
    half = CHUNK // 2
    cap = slots // n_tile
    group_rows = 2 * tiles_here
    tile_rows = n_tile * group_rows
    rows_per_ping = rows_total // ping_local
    device = a * n_tile + b
    ping_total = n_track * n_tile * ping_local
    tile_total = n_track * n_tile * tiles_here
    ping_step = n_track / ping_total
    tile_step = n_track / tile_total
    centre = 0.5 * n_track
    inside = {0: a >= 1, 2: a <= n_track - 2}

    def guarded(o, body):
        def run():
            body()
        if o == 1:
            run()
        else:
            pl.when(inside[o])(run)

    def peer(track, tile):
        return {"track": track, "tile": tile}

    def each_peer(o, act):
        def one(d, c):
            act(lax.rem(b + d, n_tile))
            return c
        lax.fori_loop(1 if o == 1 else 0, n_tile, one, 0)

    loads = [
        pltpu.make_async_copy(source, target, l_s.at[n])
        for n, (source, target) in enumerate((
            (foot_hbm, foot), (counts_hbm, counts_in), (classes_hbm, classes_in), (send_hbm, send),
            (phases_hbm, phases), (panels_hbm, panels), (weights_hbm, weights),
        ))
    ]
    for load in loads:
        load.start()

    barrier = pltpu.get_barrier_semaphore()
    for o in range(3):
        guarded(o, lambda o=o: each_peer(o, lambda s: pl.semaphore_signal(
            barrier, inc=1, device_id=peer(a + o - 1, s), device_id_type=MESH)))

    for load in loads[:5]:
        load.wait()
    entry = lax.broadcasted_iota(jnp.int32, (1, foot.shape[1]), 1)
    used = []
    for t in range(tiles_here):
        used.append(jnp.where(entry < counts_in[t], foot[t:t + 1, :], -1))
    used = jnp.concatenate(used + used, axis=0).astype(F32)
    used = used.T
    slot_lane = lax.broadcasted_iota(jnp.int32, (foot.shape[1], 3 * slots), 1).astype(F32)
    for t in range(tiles_here):
        hit = jnp.where(used[:, t:t + 1] == slot_lane, 1.0, 0.0)
        hit = jnp.max(hit, axis=0, keepdims=True) * (classes_in[t] + 1).astype(F32)
        for k in range(3):
            mark_out[k, t:t + 1, :] = hit[:, k * slots:(k + 1) * slots]
            mark_out[k, tiles_here + t:tiles_here + t + 1, :] = hit[:, k * slots:(k + 1) * slots]

    neighbours = (
        n_tile - 1
        + n_tile * (jnp.where(a >= 1, 1, 0) + jnp.where(a <= n_track - 2, 1, 0))
    )
    pl.semaphore_wait(barrier, neighbours)

    def mark_copy(k, s, slot):
        return pltpu.make_async_remote_copy(
            src_ref=mark_out.at[k], dst_ref=m_in.at[2 - k, slot],
            send_sem=m_ss.at[k, s], recv_sem=m_rs.at[2 - k, slot],
            device_id=peer(a + k - 1, s), device_id_type=MESH,
        )

    for k in (0, 2, 1):
        guarded(k, lambda k=k: each_peer(k, lambda s: mark_copy(k, s, b).start()))
    m_in[1, b] = mark_out[1]
    blank = jnp.zeros((n_tile, 2 * group_rows, half), BF16)
    for c in range(chunks):
        s_in[c, 1, b] = blank[0]
    for o in (0, 2):
        @pl.when(jnp.logical_not(inside[o]))
        def _(o=o):
            m_in[o] = jnp.zeros((n_tile, group_rows, slots), F32)
            for c in range(chunks):
                h_all[c, o] = blank
                s_in[c, 2 - o] = blank

    def ping_places(rows):
        ping = device * ping_local + rows // rows_per_ping
        return (ping.astype(F32) + 0.5) * ping_step - centre

    line = jnp.concatenate([send[n:n + 1, :] for n in range(send.shape[0])], axis=1)
    owner = line // rows_per_ping
    phase = jnp.broadcast_to(phases[...], (8, ping_local)).T[:, :1]
    ping = lax.broadcasted_iota(jnp.int32, (ping_local, 3 * slots), 0)
    angle = jnp.sum(jnp.where(ping == owner, phase, 0.0), axis=0, keepdims=True)
    sine, cosine = sincos(angle)
    place = ping_places(line)
    half_i, half_r = sincos((96.0 * half / pixels) * place)
    full_i, full_r = sincos((96.0 * CHUNK / pixels) * place)
    lines = jnp.concatenate(
        [line.astype(F32), cosine, sine, place, half_r, half_i, full_r, full_i], axis=0
    )
    column[...] = lines.T
    loads[5].wait()

    def gather(o, carry):
        mine = column[pl.ds(pl.multiple_of(o * slots, slots), slots), :]
        local = mine[:, 0:1].astype(jnp.int32)
        chosen = lax.broadcasted_iota(jnp.int32, (slots, rows_total), 1) == local
        chosen = jnp.where(chosen, 1.0, 0.0).astype(BF16)
        cosine = jnp.broadcast_to(mine[:, 1:2], (slots, CHUNK))
        sine = jnp.broadcast_to(mine[:, 2:3], (slots, CHUNK))
        for start in range(0, bins, CHUNK):
            real = jnp.dot(chosen, panels[:, start:start + CHUNK], preferred_element_type=F32)
            imag = jnp.dot(
                chosen, panels[:, bins + start:bins + start + CHUNK], preferred_element_type=F32
            )
            gath[o, :slots, start:start + CHUNK] = (cosine * real - sine * imag).astype(BF16)
            gath[o, slots:, start:start + CHUNK] = (sine * real + cosine * imag).astype(BF16)
        place = mine[:, 3:4]
        lane = lax.broadcasted_iota(jnp.int32, (slots, half), 1).astype(F32)
        across = (lane + 0.5) * (1.0 / pixels) - 0.5
        first_i, first_r = sincos(96.0 * across * place + 8.0 * (place * place))
        half_r, half_i = mine[:, 4:5], mine[:, 5:6]
        e_r[o, :, :half] = first_r
        e_i[o, :, :half] = first_i
        e_r[o, :, half:] = first_r * half_r - first_i * half_i
        e_i[o, :, half:] = first_r * half_i + first_i * half_r
        step_r[o] = jnp.broadcast_to(mine[:, 6:7], (slots, CHUNK))
        step_i[o] = jnp.broadcast_to(mine[:, 7:8], (slots, CHUNK))
        return carry

    lax.fori_loop(0, 3, gather, 0)

    for o in range(3):
        guarded(o, lambda o=o: each_peer(o, lambda s: mark_copy(2 - o, s, s).wait_recv()))
    lane = lax.broadcasted_iota(jnp.int32, (group_rows, slots), 1)
    for o in range(3):
        mark = []
        for s in range(n_tile):
            shifted = pltpu.roll(m_in[o, s], lax.rem(s - b + n_tile, n_tile) * cap, 1)
            keep = (lane >= s * cap) & (lane < (s + 1) * cap)
            mark.append(jnp.where(keep, shifted, 0.0))
        mark = jnp.concatenate(mark, axis=0)
        row = lax.broadcasted_iota(jnp.int32, (tile_rows, slots), 0)
        group = row // group_rows
        real_row = (row - group * group_rows) < tiles_here
        tile = ((a + o - 1) * n_tile + group) * tiles_here + lax.rem(row, tiles_here)
        at = (tile.astype(F32) + 0.5) * tile_step - centre
        w_i, w_r = sincos(-16.0 * at * place[:, o * slots:(o + 1) * slots])
        mark_t[o] = mark.T
        coef_t[o, :slots] = jnp.where(real_row, -w_i, w_r).T
        coef_t[o, slots:] = jnp.where(real_row, -w_r, -w_i).T
        coef = jnp.concatenate(
            [jnp.where(real_row, w_r, w_i), jnp.where(real_row, -w_i, w_r)], axis=1
        )
        mark = jnp.concatenate([mark, mark], axis=1)
        for k in range(classes):
            value = jnp.where(mark == k + 1.0, coef, 0.0)
            high = value.astype(BF16)
            om[o, k, :tile_rows] = high
            om[o, k, tile_rows:] = (value - high.astype(F32)).astype(BF16)
    q_sum[...] = jnp.zeros_like(q_sum)
    loads[6].wait()

    def s_copy(c, o, s, slot):
        return pltpu.make_async_remote_copy(
            src_ref=s_out.at[c, o, s], dst_ref=s_in.at[c, o, slot],
            send_sem=s_ss.at[c, o, s], recv_sem=s_rs.at[c, o, slot],
            device_id=peer(a + o - 1, s), device_id_type=MESH,
        )

    def h_copy(c, o, s, slot):
        return pltpu.make_async_remote_copy(
            src_ref=h_all.at[c, 1, b], dst_ref=h_all.at[c, 2 - o, slot],
            send_sem=h_ss.at[c, o, s], recv_sem=h_rs.at[c, 2 - o, slot],
            device_id=peer(a + o - 1, s), device_id_type=MESH,
        )

    def project(c):
        totals = [None, None, None]
        for k in range(classes):
            weight = weights[k, pl.ds(pl.multiple_of(c * CHUNK, CHUNK), CHUNK), :]
            y = lax.dot_general(
                gath[...].reshape(6 * slots, bins), weight, NT, preferred_element_type=F32
            )
            for o in (0, 2, 1):
                real = y[2 * o * slots:(2 * o + 1) * slots]
                imag = y[(2 * o + 1) * slots:(2 * o + 2) * slots]
                turn_r, turn_i = e_r[o], e_i[o]
                turned = jnp.concatenate(
                    [turn_r * real - turn_i * imag, turn_i * real + turn_r * imag], axis=0
                ).astype(BF16)
                z[c, o, k] = turned
                got = jnp.dot(om[o, k], turned, preferred_element_type=F32)
                totals[o] = got if k == 0 else totals[o] + got
        for o in (0, 2, 1):
            total = (totals[o][:tile_rows] + totals[o][tile_rows:]).reshape(n_tile, group_rows, CHUNK)
            if o == 1:
                part[c] = total
            s_out[c, o] = pack(total)
            guarded(o, lambda o=o: each_peer(o, lambda s: s_copy(c, o, s, b).start()))
        for o in range(3):
            now_r, now_i, by_r, by_i = e_r[o], e_i[o], step_r[o], step_i[o]
            e_r[o] = now_r * by_r - now_i * by_i
            e_i[o] = now_r * by_i + now_i * by_r

    def reduce_tiles(c):
        for o in range(3):
            guarded(2 - o, lambda o=o: each_peer(o, lambda s: s_copy(c, o, s, s).wait_recv()))
        arrived = s_in[c].reshape(3 * n_tile, 2 * group_rows, half).astype(F32)
        own = part[c, b] + unpack(jnp.sum(arrived, axis=0, keepdims=True))[0]
        s_r, s_i = own[:tiles_here], own[tiles_here:]
        power = s_r * s_r + s_i * s_i
        heavy = jnp.concatenate([power * s_r, power * s_i], axis=0)
        h_all[c, 1, b] = pack(heavy[None])[0]
        for o in (0, 2, 1):
            guarded(o, lambda o=o: each_peer(o, lambda s: h_copy(c, o, s, b).start()))
        tile_ids = device * tiles_here + lax.broadcasted_iota(jnp.int32, (tiles_here, CHUNK), 0)
        at = (tile_ids.astype(F32) + 0.5) * tile_step - centre
        pixel = c * CHUNK + lax.broadcasted_iota(jnp.int32, (tiles_here, CHUNK), 1)
        across = (pixel.astype(F32) + 0.5) * (1.0 / pixels) - 0.5
        t_i, t_r = sincos(8.0 * (at * at) - 96.0 * across * at)
        out_r = t_r * s_r - t_i * s_i
        out_i = t_i * s_r + t_r * s_i
        here = pl.ds(pl.multiple_of(c * CHUNK, CHUNK), CHUNK)
        for t in range(tiles_here):
            image[t, 0:1, here] = out_r[t:t + 1]
            image[t, 1:2, here] = out_i[t:t + 1]

    def pull(c):
        for o in (1, 0, 2):
            guarded(o, lambda o=o: each_peer(o, lambda s: h_copy(c, 2 - o, s, s).wait_recv()))
            heavy = unpack(h_all[c, o]).reshape(tile_rows, CHUNK).astype(BF16)
            q_sum[o] += lax.dot_general(
                z[c, o].reshape(classes * 2 * slots, CHUNK), heavy, NT, preferred_element_type=F32
            )

    def stage(i, carry):
        for lag, act in enumerate((project, reduce_tiles, pull)):
            @pl.when((i >= lag) & (i < chunks + lag))
            def _(lag=lag, act=act):
                act(i - lag)
        return carry

    lax.fori_loop(0, chunks + 2, stage, 0)

    ping = lax.broadcasted_iota(jnp.int32, (slots, ping_local), 1)
    spread = jnp.zeros((slots, ping_local), F32)
    for o in range(3):
        mark = jnp.concatenate([mark_t[o], mark_t[o]], axis=0)
        total = jnp.zeros((2 * slots, tile_rows), F32)
        for k in range(classes):
            got = q_sum[o, k * 2 * slots:(k + 1) * 2 * slots]
            total = jnp.where(mark == k + 1.0, got, total)
        corr = jnp.sum(total * coef_t[o], axis=1, keepdims=True)
        corr = corr[:slots] + corr[slots:]
        local = column[o * slots:(o + 1) * slots, 0:1].astype(jnp.int32)
        spread = spread + jnp.where(local // rows_per_ping == ping, corr, 0.0)
    gradient[...] = jnp.sum(spread, axis=0, keepdims=True)

    for k in range(3):
        guarded(k, lambda k=k: each_peer(k, lambda s: mark_copy(k, s, b).wait_send()))

    def finish(c, carry):
        for o in range(3):
            guarded(o, lambda o=o: each_peer(o, lambda s: s_copy(c, o, s, b).wait_send()))
            guarded(o, lambda o=o: each_peer(o, lambda s: h_copy(c, o, s, b).wait_send()))
        return carry

    lax.fori_loop(0, chunks, finish, 0)


def on_device(
    panels, phases, weight_tiles, tile_class, send_slots, foot_slot, foot_ping, tile_counts
):
    n_track = lax.axis_size("track")
    n_tile = lax.axis_size("tile")
    ping_local = phases.shape[0]
    rows_total, width = panels.shape
    bins = width // 2
    tiles_here, foot = foot_slot.shape
    classes, pixels, _ = weight_tiles.shape
    slots = send_slots.shape[0] // 3
    group_rows = 2 * tiles_here
    tile_rows = n_tile * group_rows
    chunks = pixels // CHUNK
    packed = (n_tile, 2 * group_rows, CHUNK // 2)
    vmem = pl.BlockSpec(memory_space=pltpu.VMEM)
    hbm = pl.BlockSpec(memory_space=pl.ANY)
    dma = pltpu.SemaphoreType.DMA
    image, gradient = pl.pallas_call(
        functools.partial(kernel, n_track, n_tile, tiles_here, ping_local, slots),
        out_shape=(
            jax.ShapeDtypeStruct((tiles_here, 2, pixels), F32),
            jax.ShapeDtypeStruct((1, ping_local), F32),
        ),
        in_specs=[hbm] * 7,
        out_specs=(vmem, vmem),
        scratch_shapes=[
            pltpu.SMEM((tiles_here,), jnp.int32),
            pltpu.SMEM((tiles_here,), jnp.int32),
            pltpu.VMEM((rows_total, width), BF16),
            pltpu.VMEM((1, ping_local), F32),
            pltpu.VMEM((classes, pixels, bins), BF16),
            pltpu.VMEM((3 * slots // 128, 128), jnp.int32),
            pltpu.VMEM((tiles_here, foot), jnp.int32),
            pltpu.VMEM((3 * slots, 8), F32),
            pltpu.VMEM((3, 2 * slots, bins), BF16),
            pltpu.VMEM((3, slots, CHUNK), F32),
            pltpu.VMEM((3, slots, CHUNK), F32),
            pltpu.VMEM((3, slots, CHUNK), F32),
            pltpu.VMEM((3, slots, CHUNK), F32),
            pltpu.VMEM((chunks, 3, classes, 2 * slots, CHUNK), BF16),
            pltpu.VMEM((3, classes, 2 * tile_rows, 2 * slots), BF16),
            pltpu.VMEM((3, 2 * slots, tile_rows), F32),
            pltpu.VMEM((3, slots, tile_rows), F32),
            pltpu.VMEM((3, classes * 2 * slots, tile_rows), F32),
            pltpu.VMEM((3, group_rows, slots), F32),
            pltpu.VMEM((3, n_tile, group_rows, slots), F32),
            pltpu.VMEM((chunks, n_tile, group_rows, CHUNK), F32),
            pltpu.VMEM((chunks, 3) + packed, BF16),
            pltpu.VMEM((chunks, 3) + packed, BF16),
            pltpu.VMEM((chunks, 3) + packed, BF16),
            dma((7,)),
            dma((3, n_tile)), dma((3, n_tile)),
            dma((chunks, 3, n_tile)), dma((chunks, 3, n_tile)),
            dma((chunks, 3, n_tile)), dma((chunks, 3, n_tile)),
        ],
        compiler_params=pltpu.CompilerParams(
            collective_id=0, has_side_effects=True, vmem_limit_bytes=56 * 1024 * 1024
        ),
    )(
        tile_class, tile_counts, panels, phases.reshape(1, ping_local), weight_tiles,
        send_slots.reshape(3 * slots // 128, 128), foot_slot,
    )
    return image, gradient.reshape(ping_local)


def solution(mesh):
    in_specs = (
        P(("track", "tile"), None),
        P(("track", "tile")),
        P(),
        P(("track", "tile")),
        P(("track", "tile")),
        P(("track", "tile"), None),
        P(("track", "tile"), None),
        P(("track", "tile")),
    )
    out_specs = (P(("track", "tile"), None, None), P(("track", "tile")))
    return jax.shard_map(
        on_device, mesh=mesh, in_specs=in_specs, out_specs=out_specs, check_vma=False
    )
```

```python
import functools

import jax
import jax.numpy as jnp
from jax import lax
from jax.experimental import pallas as pl
from jax.experimental.pallas import tpu as pltpu
from jax.sharding import PartitionSpec as P

F32 = jnp.float32
BF16 = jnp.bfloat16
MESH = pl.DeviceIdType.MESH
CHUNK = 256
NT = (((1,), (1,)), ((), ()))


def sincos(x):
    q = jnp.floor(x * 0.6366197723675814 + 0.5)
    r = ((x - q * 1.5703125) - q * 4.837512969970703e-4) - q * 7.549789948768648e-8
    r2 = r * r
    s = r + r * r2 * (-1.6666654611e-1 + r2 * (8.3321608736e-3 + r2 * -1.9515295891e-4))
    c = 1.0 - 0.5 * r2 + r2 * r2 * (
        4.166664568298827e-2 + r2 * (-1.388731625493765e-3 + r2 * 2.443315711809948e-5)
    )
    n = q.astype(jnp.int32)
    odd = (n & 1) == 1
    sine = jnp.where(odd, c, s)
    cosine = jnp.where(odd, s, c)
    sine = jnp.where((n & 2) == 2, -sine, sine)
    cosine = jnp.where(((n + 1) & 2) == 2, -cosine, cosine)
    return sine, cosine


def pack(block):
    half = block.shape[2] // 2
    return jnp.concatenate([block[:, :, :half], block[:, :, half:]], axis=1).astype(BF16)


def unpack(block):
    wide = block.astype(F32)
    rows = wide.shape[1] // 2
    return jnp.concatenate([wide[:, :rows], wide[:, rows:]], axis=2)


def kernel(
    n_track, n_tile, tiles_here, ping_local, slots,
    classes_hbm, counts_hbm, panels_hbm, phases_hbm, weights_hbm, send_hbm, foot_hbm,
    image, gradient,
    classes_in, counts_in, panels, phases, weights, send, foot,
    column, gath, e_r, e_i, step_r, step_i, z, om, q_coef, q_sum, marks, mark_out, m_near, m_out, m_in,
    part, near_out, near_in, tile_out, tile_in, h_all,
    l_s, n_ss, n_rs, m_ss, m_rs, b_ss, b_rs, c_ss, c_rs, d_ss, d_rs, e_ss, e_rs,
):
    a = lax.axis_index("track")
    b = lax.axis_index("tile")
    rows_total, width = panels.shape
    bins = width // 2
    classes, pixels, _ = weights.shape
    chunks = pixels // CHUNK
    half = CHUNK // 2
    cap = slots // n_tile
    group_rows = 2 * tiles_here
    tile_rows = n_tile * group_rows
    mark_rows = m_out.shape[0]
    rows_per_ping = rows_total // ping_local
    device = a * n_tile + b
    ping_total = n_track * n_tile * ping_local
    tile_total = n_track * n_tile * tiles_here
    ping_step = n_track / ping_total
    tile_step = n_track / tile_total
    centre = 0.5 * n_track
    inside = {0: a >= 1, 2: a <= n_track - 2}

    def guarded(o, body):
        def run():
            body()
        if o == 1:
            run()
        else:
            pl.when(inside[o])(run)

    def peer(track, tile):
        return {"track": track, "tile": tile}

    def each_peer(o, act):
        def one(d, c):
            act(lax.rem(b + d, n_tile))
            return c
        lax.fori_loop(1 if o == 1 else 0, n_tile, one, 0)

    loads = [
        pltpu.make_async_copy(source, target, l_s.at[n])
        for n, (source, target) in enumerate((
            (foot_hbm, foot), (counts_hbm, counts_in), (classes_hbm, classes_in), (send_hbm, send),
            (phases_hbm, phases), (panels_hbm, panels), (weights_hbm, weights),
        ))
    ]
    for load in loads:
        load.start()

    barrier = pltpu.get_barrier_semaphore()
    for o in range(3):
        guarded(o, lambda o=o: each_peer(o, lambda s: pl.semaphore_signal(
            barrier, inc=1, device_id=peer(a + o - 1, s), device_id_type=MESH)))

    for load in loads[:5]:
        load.wait()
    entry = lax.broadcasted_iota(jnp.int32, (1, foot.shape[1]), 1)
    used = []
    for t in range(tiles_here):
        used.append(jnp.where(entry < counts_in[t], foot[t:t + 1, :], -1))
    used = jnp.concatenate(used + used, axis=0).astype(F32)
    used = used.T
    slot_lane = lax.broadcasted_iota(jnp.int32, (foot.shape[1], 3 * slots), 1).astype(F32)
    for t in range(tiles_here):
        hit = jnp.where(used[:, t:t + 1] == slot_lane, 1.0, 0.0)
        hit = jnp.max(hit, axis=0, keepdims=True) * (classes_in[t] + 1).astype(F32)
        for k in range(3):
            mark_out[k, t:t + 1, :] = hit[:, k * slots:(k + 1) * slots]
            mark_out[k, tiles_here + t:tiles_here + t + 1, :] = hit[:, k * slots:(k + 1) * slots]

    neighbours = (
        n_tile - 1
        + n_tile * (jnp.where(a >= 1, 1, 0) + jnp.where(a <= n_track - 2, 1, 0))
    )
    pl.semaphore_wait(barrier, neighbours)

    def mark_step(k):
        return pltpu.make_async_remote_copy(
            src_ref=mark_out.at[k], dst_ref=m_near.at[2 - k],
            send_sem=n_ss.at[k], recv_sem=n_rs.at[2 - k],
            device_id=peer(a + k - 1, b), device_id_type=MESH,
        )

    def mark_copy(s, slot):
        return pltpu.make_async_remote_copy(
            src_ref=m_out, dst_ref=m_in.at[slot],
            send_sem=m_ss.at[s], recv_sem=m_rs.at[slot],
            device_id=peer(a, s), device_id_type=MESH,
        )

    for k in (0, 2):
        guarded(k, lambda k=k: mark_step(k).start())
    m_near[1] = mark_out[1]
    blank = jnp.zeros((n_tile, 2 * group_rows, half), BF16)
    for c in range(chunks):
        tile_in[c, b] = blank[0]
    for o in (0, 2):
        @pl.when(jnp.logical_not(inside[o]))
        def _(o=o):
            m_near[o] = jnp.zeros((group_rows, slots), F32)
            for c in range(chunks):
                h_all[c, o] = blank

    def ping_places(rows):
        ping = device * ping_local + rows // rows_per_ping
        return (ping.astype(F32) + 0.5) * ping_step - centre

    line = jnp.concatenate([send[n:n + 1, :] for n in range(send.shape[0])], axis=1)
    owner = line // rows_per_ping
    phase = jnp.broadcast_to(phases[...], (8, ping_local)).T[:, :1]
    ping = lax.broadcasted_iota(jnp.int32, (ping_local, 3 * slots), 0)
    angle = jnp.sum(jnp.where(ping == owner, phase, 0.0), axis=0, keepdims=True)
    sine, cosine = sincos(angle)
    place = ping_places(line)
    half_i, half_r = sincos((96.0 * half / pixels) * place)
    full_i, full_r = sincos((96.0 * CHUNK / pixels) * place)
    lines = jnp.concatenate(
        [line.astype(F32), cosine, sine, place, half_r, half_i, full_r, full_i], axis=0
    )
    column[...] = lines.T
    loads[5].wait()

    def gather(o, carry):
        mine = column[pl.ds(pl.multiple_of(o * slots, slots), slots), :]
        local = mine[:, 0:1].astype(jnp.int32)
        chosen = lax.broadcasted_iota(jnp.int32, (slots, rows_total), 1) == local
        chosen = jnp.where(chosen, 1.0, 0.0).astype(BF16)
        cosine = jnp.broadcast_to(mine[:, 1:2], (slots, CHUNK))
        sine = jnp.broadcast_to(mine[:, 2:3], (slots, CHUNK))
        for start in range(0, bins, CHUNK):
            real = jnp.dot(chosen, panels[:, start:start + CHUNK], preferred_element_type=F32)
            imag = jnp.dot(
                chosen, panels[:, bins + start:bins + start + CHUNK], preferred_element_type=F32
            )
            gath[o, :slots, start:start + CHUNK] = (cosine * real - sine * imag).astype(BF16)
            gath[o, slots:, start:start + CHUNK] = (sine * real + cosine * imag).astype(BF16)
        place = mine[:, 3:4]
        lane = lax.broadcasted_iota(jnp.int32, (slots, half), 1).astype(F32)
        across = (lane + 0.5) * (1.0 / pixels) - 0.5
        first_i, first_r = sincos(96.0 * across * place + 8.0 * (place * place))
        half_r, half_i = mine[:, 4:5], mine[:, 5:6]
        e_r[o, :, :half] = first_r
        e_i[o, :, :half] = first_i
        e_r[o, :, half:] = first_r * half_r - first_i * half_i
        e_i[o, :, half:] = first_r * half_i + first_i * half_r
        step_r[o] = jnp.broadcast_to(mine[:, 6:7], (slots, CHUNK))
        step_i[o] = jnp.broadcast_to(mine[:, 7:8], (slots, CHUNK))
        return carry

    gather(0, 0)
    for o in (0, 2):
        guarded(o, lambda o=o: mark_step(2 - o).wait_recv())
    near = [m_near[o, :tiles_here] for o in range(3)]
    near = jnp.concatenate(near + [jnp.zeros((mark_rows - 3 * tiles_here, slots), F32)], axis=0)
    m_out[...] = near.astype(BF16)
    m_in[b] = near.astype(BF16)
    each_peer(1, lambda s: mark_copy(s, b).start())
    lax.fori_loop(1, 3, gather, 0)

    each_peer(1, lambda s: mark_copy(s, s).wait_recv())
    lane = lax.broadcasted_iota(jnp.int32, (mark_rows, slots), 1)
    got_marks = []
    for s in range(n_tile):
        shifted = pltpu.roll(m_in[s].astype(F32), lax.rem(s - b + n_tile, n_tile) * cap, 1)
        got_marks.append(jnp.where((lane >= s * cap) & (lane < (s + 1) * cap), shifted, 0.0))
    for o in range(3):
        mark = []
        for s in range(n_tile):
            rows = got_marks[s][o * tiles_here:(o + 1) * tiles_here]
            mark += [rows, rows]
        mark = jnp.concatenate(mark, axis=0)
        row = lax.broadcasted_iota(jnp.int32, (tile_rows, slots), 0)
        group = row // group_rows
        real_row = (row - group * group_rows) < tiles_here
        tile = ((a + o - 1) * n_tile + group) * tiles_here + lax.rem(row, tiles_here)
        at = (tile.astype(F32) + 0.5) * tile_step - centre
        w_i, w_r = sincos(-16.0 * at * place[:, o * slots:(o + 1) * slots])
        marks[o, :, :slots] = mark
        marks[o, :, slots:] = mark
        q_coef[o, :, :slots] = jnp.where(real_row, -w_i, w_r)
        q_coef[o, :, slots:] = jnp.where(real_row, -w_r, -w_i)
        coef = jnp.concatenate(
            [jnp.where(real_row, w_r, w_i), jnp.where(real_row, -w_i, w_r)], axis=1
        )
        mark = jnp.concatenate([mark, mark], axis=1)
        for k in range(classes):
            value = jnp.where(mark == k + 1.0, coef, 0.0)
            high = value.astype(BF16)
            om[o, k, :tile_rows] = high
            om[o, k, tile_rows:] = (value - high.astype(F32)).astype(BF16)
    q_sum[...] = jnp.zeros_like(q_sum)
    loads[6].wait()

    def near_copy(c, j):
        return pltpu.make_async_remote_copy(
            src_ref=near_out.at[c, j], dst_ref=near_in.at[c, j],
            send_sem=b_ss.at[c, j], recv_sem=b_rs.at[c, j],
            device_id=peer(a + 2 * j - 1, b), device_id_type=MESH,
        )

    def tile_copy(c, s, slot):
        return pltpu.make_async_remote_copy(
            src_ref=tile_out.at[c, s], dst_ref=tile_in.at[c, slot],
            send_sem=c_ss.at[c, s], recv_sem=c_rs.at[c, slot],
            device_id=peer(a, s), device_id_type=MESH,
        )

    def h_copy(c, s, slot):
        return pltpu.make_async_remote_copy(
            src_ref=h_all.at[c, 1, b], dst_ref=h_all.at[c, 1, slot],
            send_sem=d_ss.at[c, s], recv_sem=d_rs.at[c, slot],
            device_id=peer(a, s), device_id_type=MESH,
        )

    def h_forward(c, o):
        return pltpu.make_async_remote_copy(
            src_ref=h_all.at[c, 1], dst_ref=h_all.at[c, 2 - o],
            send_sem=e_ss.at[c, o // 2], recv_sem=e_rs.at[c, o // 2],
            device_id=peer(a + o - 1, b), device_id_type=MESH,
        )

    def project(c):
        totals = [None, None, None]
        for k in range(classes):
            weight = weights[k, pl.ds(pl.multiple_of(c * CHUNK, CHUNK), CHUNK), :]
            for o in (0, 2, 1):
                y = lax.dot_general(gath[o], weight, NT, preferred_element_type=F32)
                turn_r, turn_i = e_r[o], e_i[o]
                turned = jnp.concatenate(
                    [turn_r * y[:slots] - turn_i * y[slots:], turn_i * y[:slots] + turn_r * y[slots:]],
                    axis=0,
                ).astype(BF16)
                z[c, o, k] = turned
                got = jnp.dot(om[o, k], turned, preferred_element_type=F32)
                totals[o] = got if k == 0 else totals[o] + got
        for o in range(3):
            total = (totals[o][:tile_rows] + totals[o][tile_rows:]).reshape(n_tile, group_rows, CHUNK)
            if o == 1:
                part[c] = total
            else:
                near_out[c, o // 2] = pack(total)
        for o in (0, 2):
            guarded(o, lambda o=o: near_copy(c, o // 2).start())
        for o in range(3):
            now_r, now_i, by_r, by_i = e_r[o], e_i[o], step_r[o], step_i[o]
            e_r[o] = now_r * by_r - now_i * by_i
            e_i[o] = now_r * by_i + now_i * by_r

    def reduce_tracks(c):
        for j in range(2):
            def add(j=j):
                near_copy(c, j).wait_recv()
                part[c] += unpack(near_in[c, j])
            guarded(2 - 2 * j, add)
        tile_out[c] = pack(part[c])
        each_peer(1, lambda s: tile_copy(c, s, b).start())

    def reduce_tiles(c):
        each_peer(1, lambda s: tile_copy(c, s, s).wait_recv())
        arrived = unpack(tile_in[c])
        own = part[c, b]
        for s in range(n_tile):
            own = own + arrived[s]
        s_r, s_i = own[:tiles_here], own[tiles_here:]
        power = s_r * s_r + s_i * s_i
        heavy = jnp.concatenate([power * s_r, power * s_i], axis=0)
        h_all[c, 1, b] = pack(heavy[None])[0]
        each_peer(1, lambda s: h_copy(c, s, b).start())
        tile_ids = device * tiles_here + lax.broadcasted_iota(jnp.int32, (tiles_here, CHUNK), 0)
        at = (tile_ids.astype(F32) + 0.5) * tile_step - centre
        pixel = c * CHUNK + lax.broadcasted_iota(jnp.int32, (tiles_here, CHUNK), 1)
        across = (pixel.astype(F32) + 0.5) * (1.0 / pixels) - 0.5
        t_i, t_r = sincos(8.0 * (at * at) - 96.0 * across * at)
        out_r = t_r * s_r - t_i * s_i
        out_i = t_i * s_r + t_r * s_i
        here = pl.ds(pl.multiple_of(c * CHUNK, CHUNK), CHUNK)
        for t in range(tiles_here):
            image[t, 0:1, here] = out_r[t:t + 1]
            image[t, 1:2, here] = out_i[t:t + 1]

    def relay(c):
        each_peer(1, lambda s: h_copy(c, s, s).wait_recv())
        for o in (0, 2):
            guarded(o, lambda o=o: h_forward(c, o).start())

    def pull(c):
        for o in (1, 0, 2):
            if o != 1:
                guarded(o, lambda o=o: h_forward(c, 2 - o).wait_recv())
            heavy = unpack(h_all[c, o]).reshape(tile_rows, CHUNK).astype(BF16)
            mark = marks[o]
            total = jnp.zeros((tile_rows, 2 * slots), F32)
            for k in range(classes):
                got = lax.dot_general(heavy, z[c, o, k], NT, preferred_element_type=F32)
                total = jnp.where(mark == k + 1.0, got, total)
            q_sum[o] += total

    def stage(i, carry):
        for lag, act in enumerate((project, reduce_tracks, reduce_tiles, relay, pull)):
            @pl.when((i >= lag) & (i < chunks + lag))
            def _(lag=lag, act=act):
                act(i - lag)
        return carry

    lax.fori_loop(0, chunks + 4, stage, 0)

    ping = lax.broadcasted_iota(jnp.int32, (ping_local, slots), 0)
    spread = jnp.zeros((ping_local, slots), F32)
    for o in range(3):
        corr = jnp.sum(q_sum[o] * q_coef[o], axis=0, keepdims=True)
        corr = corr[:, :slots] + corr[:, slots:]
        mine = line[:, o * slots:(o + 1) * slots]
        spread = spread + jnp.where(mine // rows_per_ping == ping, corr, 0.0)
    sums = jnp.sum(spread, axis=1, keepdims=True)
    gradient[...] = jnp.broadcast_to(sums, (ping_local, 128)).T[:1]

    for k in (0, 2):
        guarded(k, lambda k=k: mark_step(k).wait_send())
    each_peer(1, lambda s: mark_copy(s, b).wait_send())

    def finish(c, carry):
        for o in (0, 2):
            def sent(o=o):
                near_copy(c, o // 2).wait_send()
                h_forward(c, o).wait_send()
            guarded(o, sent)
        each_peer(1, lambda s: tile_copy(c, s, b).wait_send())
        each_peer(1, lambda s: h_copy(c, s, b).wait_send())
        return carry

    lax.fori_loop(0, chunks, finish, 0)


def on_device(
    panels, phases, weight_tiles, tile_class, send_slots, foot_slot, foot_ping, tile_counts
):
    n_track = lax.axis_size("track")
    n_tile = lax.axis_size("tile")
    ping_local = phases.shape[0]
    rows_total, width = panels.shape
    bins = width // 2
    tiles_here, foot = foot_slot.shape
    classes, pixels, _ = weight_tiles.shape
    slots = send_slots.shape[0] // 3
    group_rows = 2 * tiles_here
    tile_rows = n_tile * group_rows
    chunks = pixels // CHUNK
    mark_rows = -(-3 * tiles_here // 16) * 16
    packed = (n_tile, 2 * group_rows, CHUNK // 2)
    vmem = pl.BlockSpec(memory_space=pltpu.VMEM)
    hbm = pl.BlockSpec(memory_space=pltpu.HBM)
    dma = pltpu.SemaphoreType.DMA
    image, gradient = pl.pallas_call(
        functools.partial(kernel, n_track, n_tile, tiles_here, ping_local, slots),
        out_shape=(
            jax.ShapeDtypeStruct((tiles_here, 2, pixels), F32),
            jax.ShapeDtypeStruct((1, ping_local), F32),
        ),
        in_specs=[hbm] * 7,
        out_specs=(vmem, vmem),
        scratch_shapes=[
            pltpu.SMEM((tiles_here,), jnp.int32),
            pltpu.SMEM((tiles_here,), jnp.int32),
            pltpu.VMEM((rows_total, width), BF16),
            pltpu.VMEM((1, ping_local), F32),
            pltpu.VMEM((classes, pixels, bins), BF16),
            pltpu.VMEM((3 * slots // 128, 128), jnp.int32),
            pltpu.VMEM((tiles_here, foot), jnp.int32),
            pltpu.VMEM((3 * slots, 8), F32),
            pltpu.VMEM((3, 2 * slots, bins), BF16),
            pltpu.VMEM((3, slots, CHUNK), F32),
            pltpu.VMEM((3, slots, CHUNK), F32),
            pltpu.VMEM((3, slots, CHUNK), F32),
            pltpu.VMEM((3, slots, CHUNK), F32),
            pltpu.VMEM((chunks, 3, classes, 2 * slots, CHUNK), BF16),
            pltpu.VMEM((3, classes, 2 * tile_rows, 2 * slots), BF16),
            pltpu.VMEM((3, tile_rows, 2 * slots), F32),
            pltpu.VMEM((3, tile_rows, 2 * slots), F32),
            pltpu.VMEM((3, tile_rows, 2 * slots), F32),
            pltpu.VMEM((3, group_rows, slots), F32),
            pltpu.VMEM((3, group_rows, slots), F32),
            pltpu.VMEM((mark_rows, slots), BF16),
            pltpu.VMEM((n_tile, mark_rows, slots), BF16),
            pltpu.VMEM((chunks, n_tile, group_rows, CHUNK), F32),
            pltpu.VMEM((chunks, 2) + packed, BF16),
            pltpu.VMEM((chunks, 2) + packed, BF16),
            pltpu.VMEM((chunks,) + packed, BF16),
            pltpu.VMEM((chunks,) + packed, BF16),
            pltpu.VMEM((chunks, 3) + packed, BF16),
            dma((7,)),
            dma((3,)), dma((3,)),
            dma((n_tile,)), dma((n_tile,)),
            dma((chunks, 2)), dma((chunks, 2)),
            dma((chunks, n_tile)), dma((chunks, n_tile)),
            dma((chunks, n_tile)), dma((chunks, n_tile)),
            dma((chunks, 2)), dma((chunks, 2)),
        ],
        compiler_params=pltpu.CompilerParams(
            collective_id=0, has_side_effects=True, vmem_limit_bytes=48 * 1024 * 1024
        ),
    )(
        tile_class, tile_counts, panels, phases.reshape(1, ping_local), weight_tiles,
        send_slots.reshape(3 * slots // 128, 128), foot_slot,
    )
    return image, gradient.reshape(ping_local)


def solution(mesh):
    in_specs = (
        P(("track", "tile"), None),
        P(("track", "tile")),
        P(),
        P(("track", "tile")),
        P(("track", "tile")),
        P(("track", "tile"), None),
        P(("track", "tile"), None),
        P(("track", "tile")),
    )
    out_specs = (P(("track", "tile"), None, None), P(("track", "tile")))
    return jax.shard_map(
        on_device, mesh=mesh, in_specs=in_specs, out_specs=out_specs, check_vma=False
    )
```

```python
import functools

import jax
import jax.numpy as jnp
from jax import lax
from jax.experimental import pallas as pl
from jax.experimental.pallas import tpu as pltpu
from jax.sharding import PartitionSpec as P

F32 = jnp.float32
BF16 = jnp.bfloat16
MESH = pl.DeviceIdType.MESH
CHUNK = 256
NT = (((1,), (1,)), ((), ()))


def sincos(x):
    q = jnp.floor(x * 0.6366197723675814 + 0.5)
    r = ((x - q * 1.5703125) - q * 4.837512969970703e-4) - q * 7.549789948768648e-8
    r2 = r * r
    s = r + r * r2 * (-1.6666654611e-1 + r2 * (8.3321608736e-3 + r2 * -1.9515295891e-4))
    c = 1.0 - 0.5 * r2 + r2 * r2 * (
        4.166664568298827e-2 + r2 * (-1.388731625493765e-3 + r2 * 2.443315711809948e-5)
    )
    n = q.astype(jnp.int32)
    odd = (n & 1) == 1
    sine = jnp.where(odd, c, s)
    cosine = jnp.where(odd, s, c)
    sine = jnp.where((n & 2) == 2, -sine, sine)
    cosine = jnp.where(((n + 1) & 2) == 2, -cosine, cosine)
    return sine, cosine


def pack(block):
    half = block.shape[2] // 2
    return jnp.concatenate([block[:, :, :half], block[:, :, half:]], axis=1).astype(BF16)


def unpack(block):
    wide = block.astype(F32)
    rows = wide.shape[1] // 2
    return jnp.concatenate([wide[:, :rows], wide[:, rows:]], axis=2)


def kernel(
    n_track, n_tile, tiles_here, ping_local, slots,
    classes_hbm, counts_hbm, panels_hbm, phases_hbm, weights_hbm, send_hbm, foot_hbm,
    image, gradient,
    classes_in, counts_in, panels, phases, weights, send, foot,
    column, gath, e_r, e_i, step_r, step_i, z, om, q_coef, q_sum, marks, mark_out, m_near, m_out, m_in,
    part, near_out, near_in, tile_out, tile_in, h_all,
    l_s, n_ss, n_rs, m_ss, m_rs, b_ss, b_rs, c_ss, c_rs, d_ss, d_rs, e_ss, e_rs,
):
    a = lax.axis_index("track")
    b = lax.axis_index("tile")
    rows_total, width = panels.shape
    bins = width // 2
    classes, pixels, _ = weights.shape
    chunks = pixels // CHUNK
    half = CHUNK // 2
    cap = slots // n_tile
    group_rows = 2 * tiles_here
    tile_rows = n_tile * group_rows
    mark_rows = m_out.shape[0]
    rows_per_ping = rows_total // ping_local
    device = a * n_tile + b
    ping_total = n_track * n_tile * ping_local
    tile_total = n_track * n_tile * tiles_here
    ping_step = n_track / ping_total
    tile_step = n_track / tile_total
    centre = 0.5 * n_track
    inside = {0: a >= 1, 2: a <= n_track - 2}

    def guarded(o, body):
        def run():
            body()
        if o == 1:
            run()
        else:
            pl.when(inside[o])(run)

    def peer(track, tile):
        return {"track": track, "tile": tile}

    def each_peer(o, act):
        for d in range(1 if o == 1 else 0, n_tile):
            act(lax.rem(b + d, n_tile))

    loads = [
        pltpu.make_async_copy(source, target, l_s.at[n])
        for n, (source, target) in enumerate((
            (foot_hbm, foot), (counts_hbm, counts_in), (classes_hbm, classes_in), (send_hbm, send),
            (phases_hbm, phases), (panels_hbm, panels), (weights_hbm, weights),
        ))
    ]
    for load in loads:
        load.start()

    barrier = pltpu.get_barrier_semaphore()
    for o in range(3):
        guarded(o, lambda o=o: each_peer(o, lambda s: pl.semaphore_signal(
            barrier, inc=1, device_id=peer(a + o - 1, s), device_id_type=MESH)))

    for load in loads[:5]:
        load.wait()
    entry = lax.broadcasted_iota(jnp.int32, (1, foot.shape[1]), 1)
    used = []
    for t in range(tiles_here):
        used.append(jnp.where(entry < counts_in[t], foot[t:t + 1, :], -1))
    used = jnp.concatenate(used + used, axis=0).astype(F32)
    used = used.T
    slot_lane = lax.broadcasted_iota(jnp.int32, (foot.shape[1], 3 * slots), 1).astype(F32)
    for t in range(tiles_here):
        hit = jnp.where(used[:, t:t + 1] == slot_lane, 1.0, 0.0)
        hit = jnp.max(hit, axis=0, keepdims=True) * (classes_in[t] + 1).astype(F32)
        for k in range(3):
            mark_out[k, t:t + 1, :] = hit[:, k * slots:(k + 1) * slots]
            mark_out[k, tiles_here + t:tiles_here + t + 1, :] = hit[:, k * slots:(k + 1) * slots]

    neighbours = (
        n_tile - 1
        + n_tile * (jnp.where(a >= 1, 1, 0) + jnp.where(a <= n_track - 2, 1, 0))
    )
    pl.semaphore_wait(barrier, neighbours)

    def mark_step(k):
        return pltpu.make_async_remote_copy(
            src_ref=mark_out.at[k], dst_ref=m_near.at[2 - k],
            send_sem=n_ss.at[k], recv_sem=n_rs.at[2 - k],
            device_id=peer(a + k - 1, b), device_id_type=MESH,
        )

    def mark_copy(s, slot):
        return pltpu.make_async_remote_copy(
            src_ref=m_out, dst_ref=m_in.at[slot],
            send_sem=m_ss.at[s], recv_sem=m_rs.at[slot],
            device_id=peer(a, s), device_id_type=MESH,
        )

    for k in (0, 2):
        guarded(k, lambda k=k: mark_step(k).start())
    m_near[1] = mark_out[1]
    blank = jnp.zeros((n_tile, 2 * group_rows, half), BF16)
    for c in range(chunks):
        tile_in[c, b] = blank[0]
    for o in (0, 2):
        @pl.when(jnp.logical_not(inside[o]))
        def _(o=o):
            m_near[o] = jnp.zeros((group_rows, slots), F32)
            for c in range(chunks):
                h_all[c, o] = blank

    def ping_places(rows):
        ping = device * ping_local + rows // rows_per_ping
        return (ping.astype(F32) + 0.5) * ping_step - centre

    line = jnp.concatenate([send[n:n + 1, :] for n in range(send.shape[0])], axis=1)
    owner = line // rows_per_ping
    phase = jnp.broadcast_to(phases[...], (8, ping_local)).T[:, :1]
    ping = lax.broadcasted_iota(jnp.int32, (ping_local, 3 * slots), 0)
    angle = jnp.sum(jnp.where(ping == owner, phase, 0.0), axis=0, keepdims=True)
    sine, cosine = sincos(angle)
    place = ping_places(line)
    half_i, half_r = sincos((96.0 * half / pixels) * place)
    full_i, full_r = sincos((96.0 * CHUNK / pixels) * place)
    lines = jnp.concatenate(
        [line.astype(F32), cosine, sine, place, half_r, half_i, full_r, full_i], axis=0
    )
    column[...] = lines.T
    loads[5].wait()

    def gather(o, carry):
        mine = column[pl.ds(pl.multiple_of(o * slots, slots), slots), :]
        local = mine[:, 0:1].astype(jnp.int32)
        chosen = lax.broadcasted_iota(jnp.int32, (slots, rows_total), 1) == local
        chosen = jnp.where(chosen, 1.0, 0.0).astype(BF16)
        cosine = jnp.broadcast_to(mine[:, 1:2], (slots, CHUNK))
        sine = jnp.broadcast_to(mine[:, 2:3], (slots, CHUNK))
        for start in range(0, bins, CHUNK):
            real = jnp.dot(chosen, panels[:, start:start + CHUNK], preferred_element_type=F32)
            imag = jnp.dot(
                chosen, panels[:, bins + start:bins + start + CHUNK], preferred_element_type=F32
            )
            gath[o, :slots, start:start + CHUNK] = (cosine * real - sine * imag).astype(BF16)
            gath[o, slots:, start:start + CHUNK] = (sine * real + cosine * imag).astype(BF16)
        place = mine[:, 3:4]
        lane = lax.broadcasted_iota(jnp.int32, (slots, half), 1).astype(F32)
        across = (lane + 0.5) * (1.0 / pixels) - 0.5
        first_i, first_r = sincos(96.0 * across * place + 8.0 * (place * place))
        half_r, half_i = mine[:, 4:5], mine[:, 5:6]
        e_r[o, :, :half] = first_r
        e_i[o, :, :half] = first_i
        e_r[o, :, half:] = first_r * half_r - first_i * half_i
        e_i[o, :, half:] = first_r * half_i + first_i * half_r
        step_r[o] = jnp.broadcast_to(mine[:, 6:7], (slots, CHUNK))
        step_i[o] = jnp.broadcast_to(mine[:, 7:8], (slots, CHUNK))
        return carry

    gather(0, 0)
    for o in (0, 2):
        guarded(o, lambda o=o: mark_step(2 - o).wait_recv())
    near = [m_near[o, :tiles_here] for o in range(3)]
    near = jnp.concatenate(near + [jnp.zeros((mark_rows - 3 * tiles_here, slots), F32)], axis=0)
    m_out[...] = near.astype(BF16)
    m_in[b] = near.astype(BF16)
    each_peer(1, lambda s: mark_copy(s, b).start())
    lax.fori_loop(1, 3, gather, 0)

    each_peer(1, lambda s: mark_copy(s, s).wait_recv())
    lane = lax.broadcasted_iota(jnp.int32, (mark_rows, slots), 1)
    got_marks = []
    for s in range(n_tile):
        shifted = pltpu.roll(m_in[s].astype(F32), lax.rem(s - b + n_tile, n_tile) * cap, 1)
        got_marks.append(jnp.where((lane >= s * cap) & (lane < (s + 1) * cap), shifted, 0.0))
    for o in range(3):
        mark = []
        for s in range(n_tile):
            rows = got_marks[s][o * tiles_here:(o + 1) * tiles_here]
            mark += [rows, rows]
        mark = jnp.concatenate(mark, axis=0)
        row = lax.broadcasted_iota(jnp.int32, (tile_rows, slots), 0)
        group = row // group_rows
        real_row = (row - group * group_rows) < tiles_here
        tile = ((a + o - 1) * n_tile + group) * tiles_here + lax.rem(row, tiles_here)
        at = (tile.astype(F32) + 0.5) * tile_step - centre
        w_i, w_r = sincos(-16.0 * at * place[:, o * slots:(o + 1) * slots])
        marks[o, :, :slots] = mark
        marks[o, :, slots:] = mark
        q_coef[o, :, :slots] = jnp.where(real_row, -w_i, w_r)
        q_coef[o, :, slots:] = jnp.where(real_row, -w_r, -w_i)
        coef = jnp.concatenate(
            [jnp.where(real_row, w_r, w_i), jnp.where(real_row, -w_i, w_r)], axis=1
        )
        mark = jnp.concatenate([mark, mark], axis=1)
        for k in range(classes):
            value = jnp.where(mark == k + 1.0, coef, 0.0)
            high = value.astype(BF16)
            om[o, k, :tile_rows] = high
            om[o, k, tile_rows:] = (value - high.astype(F32)).astype(BF16)
    q_sum[...] = jnp.zeros_like(q_sum)
    loads[6].wait()

    def near_copy(c, j):
        return pltpu.make_async_remote_copy(
            src_ref=near_out.at[c, j], dst_ref=near_in.at[c, j],
            send_sem=b_ss.at[c, j], recv_sem=b_rs.at[c, j],
            device_id=peer(a + 2 * j - 1, b), device_id_type=MESH,
        )

    def tile_copy(c, s, slot):
        return pltpu.make_async_remote_copy(
            src_ref=tile_out.at[c, s], dst_ref=tile_in.at[c, slot],
            send_sem=c_ss.at[c, s], recv_sem=c_rs.at[c, slot],
            device_id=peer(a, s), device_id_type=MESH,
        )

    def h_copy(c, s, slot):
        return pltpu.make_async_remote_copy(
            src_ref=h_all.at[c, 1, b], dst_ref=h_all.at[c, 1, slot],
            send_sem=d_ss.at[c, s], recv_sem=d_rs.at[c, slot],
            device_id=peer(a, s), device_id_type=MESH,
        )

    def h_forward(c, o):
        return pltpu.make_async_remote_copy(
            src_ref=h_all.at[c, 1], dst_ref=h_all.at[c, 2 - o],
            send_sem=e_ss.at[c, o // 2], recv_sem=e_rs.at[c, o // 2],
            device_id=peer(a + o - 1, b), device_id_type=MESH,
        )

    def project(c):
        totals = [None, None, None]
        for k in range(classes):
            weight = weights[k, pl.ds(pl.multiple_of(c * CHUNK, CHUNK), CHUNK), :]
            for o in (0, 2, 1):
                y = lax.dot_general(gath[o], weight, NT, preferred_element_type=F32)
                turn_r, turn_i = e_r[o], e_i[o]
                turned = jnp.concatenate(
                    [turn_r * y[:slots] - turn_i * y[slots:], turn_i * y[:slots] + turn_r * y[slots:]],
                    axis=0,
                ).astype(BF16)
                z[c, o, k] = turned
                got = jnp.dot(om[o, k], turned, preferred_element_type=F32)
                totals[o] = got if k == 0 else totals[o] + got
        for o in range(3):
            total = (totals[o][:tile_rows] + totals[o][tile_rows:]).reshape(n_tile, group_rows, CHUNK)
            if o == 1:
                part[c] = total
            else:
                near_out[c, o // 2] = pack(total)
        for o in (0, 2):
            guarded(o, lambda o=o: near_copy(c, o // 2).start())
        for o in range(3):
            now_r, now_i, by_r, by_i = e_r[o], e_i[o], step_r[o], step_i[o]
            e_r[o] = now_r * by_r - now_i * by_i
            e_i[o] = now_r * by_i + now_i * by_r

    def reduce_tracks(c):
        for j in range(2):
            def add(j=j):
                near_copy(c, j).wait_recv()
                part[c] += unpack(near_in[c, j])
            guarded(2 - 2 * j, add)
        tile_out[c] = pack(part[c])
        each_peer(1, lambda s: tile_copy(c, s, b).start())

    def reduce_tiles(c):
        each_peer(1, lambda s: tile_copy(c, s, s).wait_recv())
        arrived = unpack(tile_in[c])
        own = part[c, b]
        for s in range(n_tile):
            own = own + arrived[s]
        s_r, s_i = own[:tiles_here], own[tiles_here:]
        power = s_r * s_r + s_i * s_i
        heavy = jnp.concatenate([power * s_r, power * s_i], axis=0)
        h_all[c, 1, b] = pack(heavy[None])[0]
        each_peer(1, lambda s: h_copy(c, s, b).start())
        tile_ids = device * tiles_here + lax.broadcasted_iota(jnp.int32, (tiles_here, CHUNK), 0)
        at = (tile_ids.astype(F32) + 0.5) * tile_step - centre
        pixel = c * CHUNK + lax.broadcasted_iota(jnp.int32, (tiles_here, CHUNK), 1)
        across = (pixel.astype(F32) + 0.5) * (1.0 / pixels) - 0.5
        t_i, t_r = sincos(8.0 * (at * at) - 96.0 * across * at)
        out_r = t_r * s_r - t_i * s_i
        out_i = t_i * s_r + t_r * s_i
        here = pl.ds(pl.multiple_of(c * CHUNK, CHUNK), CHUNK)
        for t in range(tiles_here):
            image[t, 0:1, here] = out_r[t:t + 1]
            image[t, 1:2, here] = out_i[t:t + 1]

    def relay(c):
        each_peer(1, lambda s: h_copy(c, s, s).wait_recv())
        for o in (0, 2):
            guarded(o, lambda o=o: h_forward(c, o).start())

    def pull(c):
        for o in (1, 0, 2):
            if o != 1:
                guarded(o, lambda o=o: h_forward(c, 2 - o).wait_recv())
            heavy = unpack(h_all[c, o]).reshape(tile_rows, CHUNK).astype(BF16)
            mark = marks[o]
            total = jnp.zeros((tile_rows, 2 * slots), F32)
            for k in range(classes):
                got = lax.dot_general(heavy, z[c, o, k], NT, preferred_element_type=F32)
                total = jnp.where(mark == k + 1.0, got, total)
            q_sum[o] += total

    def stage(i, carry):
        for lag, act in enumerate((project, reduce_tracks, reduce_tiles, relay, pull)):
            @pl.when((i >= lag) & (i < chunks + lag))
            def _(lag=lag, act=act):
                act(i - lag)
        return carry

    lax.fori_loop(0, chunks + 4, stage, 0)

    ping = lax.broadcasted_iota(jnp.int32, (ping_local, slots), 0)
    spread = jnp.zeros((ping_local, slots), F32)
    for o in range(3):
        corr = jnp.sum(q_sum[o] * q_coef[o], axis=0, keepdims=True)
        corr = corr[:, :slots] + corr[:, slots:]
        mine = line[:, o * slots:(o + 1) * slots]
        spread = spread + jnp.where(mine // rows_per_ping == ping, corr, 0.0)
    sums = jnp.sum(spread, axis=1, keepdims=True)
    gradient[...] = jnp.broadcast_to(sums, (ping_local, 128)).T[:1]

    for k in (0, 2):
        guarded(k, lambda k=k: mark_step(k).wait_send())
    each_peer(1, lambda s: mark_copy(s, b).wait_send())

    def finish(c, carry):
        for o in (0, 2):
            def sent(o=o):
                near_copy(c, o // 2).wait_send()
                h_forward(c, o).wait_send()
            guarded(o, sent)
        each_peer(1, lambda s: tile_copy(c, s, b).wait_send())
        each_peer(1, lambda s: h_copy(c, s, b).wait_send())
        return carry

    lax.fori_loop(0, chunks, finish, 0)


def on_device(
    panels, phases, weight_tiles, tile_class, send_slots, foot_slot, foot_ping, tile_counts
):
    n_track = lax.axis_size("track")
    n_tile = lax.axis_size("tile")
    ping_local = phases.shape[0]
    rows_total, width = panels.shape
    bins = width // 2
    tiles_here, foot = foot_slot.shape
    classes, pixels, _ = weight_tiles.shape
    slots = send_slots.shape[0] // 3
    group_rows = 2 * tiles_here
    tile_rows = n_tile * group_rows
    chunks = pixels // CHUNK
    mark_rows = -(-3 * tiles_here // 16) * 16
    packed = (n_tile, 2 * group_rows, CHUNK // 2)
    vmem = pl.BlockSpec(memory_space=pltpu.VMEM)
    hbm = pl.BlockSpec(memory_space=pltpu.HBM)
    dma = pltpu.SemaphoreType.DMA
    image, gradient = pl.pallas_call(
        functools.partial(kernel, n_track, n_tile, tiles_here, ping_local, slots),
        out_shape=(
            jax.ShapeDtypeStruct((tiles_here, 2, pixels), F32),
            jax.ShapeDtypeStruct((1, ping_local), F32),
        ),
        in_specs=[hbm] * 7,
        out_specs=(vmem, vmem),
        scratch_shapes=[
            pltpu.SMEM((tiles_here,), jnp.int32),
            pltpu.SMEM((tiles_here,), jnp.int32),
            pltpu.VMEM((rows_total, width), BF16),
            pltpu.VMEM((1, ping_local), F32),
            pltpu.VMEM((classes, pixels, bins), BF16),
            pltpu.VMEM((3 * slots // 128, 128), jnp.int32),
            pltpu.VMEM((tiles_here, foot), jnp.int32),
            pltpu.VMEM((3 * slots, 8), F32),
            pltpu.VMEM((3, 2 * slots, bins), BF16),
            pltpu.VMEM((3, slots, CHUNK), F32),
            pltpu.VMEM((3, slots, CHUNK), F32),
            pltpu.VMEM((3, slots, CHUNK), F32),
            pltpu.VMEM((3, slots, CHUNK), F32),
            pltpu.VMEM((chunks, 3, classes, 2 * slots, CHUNK), BF16),
            pltpu.VMEM((3, classes, 2 * tile_rows, 2 * slots), BF16),
            pltpu.VMEM((3, tile_rows, 2 * slots), F32),
            pltpu.VMEM((3, tile_rows, 2 * slots), F32),
            pltpu.VMEM((3, tile_rows, 2 * slots), F32),
            pltpu.VMEM((3, group_rows, slots), F32),
            pltpu.VMEM((3, group_rows, slots), F32),
            pltpu.VMEM((mark_rows, slots), BF16),
            pltpu.VMEM((n_tile, mark_rows, slots), BF16),
            pltpu.VMEM((chunks, n_tile, group_rows, CHUNK), F32),
            pltpu.VMEM((chunks, 2) + packed, BF16),
            pltpu.VMEM((chunks, 2) + packed, BF16),
            pltpu.VMEM((chunks,) + packed, BF16),
            pltpu.VMEM((chunks,) + packed, BF16),
            pltpu.VMEM((chunks, 3) + packed, BF16),
            dma((7,)),
            dma((3,)), dma((3,)),
            dma((n_tile,)), dma((n_tile,)),
            dma((chunks, 2)), dma((chunks, 2)),
            dma((chunks, n_tile)), dma((chunks, n_tile)),
            dma((chunks, n_tile)), dma((chunks, n_tile)),
            dma((chunks, 2)), dma((chunks, 2)),
        ],
        compiler_params=pltpu.CompilerParams(
            collective_id=0, has_side_effects=True, vmem_limit_bytes=56 * 1024 * 1024
        ),
    )(
        tile_class, tile_counts, panels, phases.reshape(1, ping_local), weight_tiles,
        send_slots.reshape(3 * slots // 128, 128), foot_slot,
    )
    return image, gradient.reshape(ping_local)


def solution(mesh):
    in_specs = (
        P(("track", "tile"), None),
        P(("track", "tile")),
        P(),
        P(("track", "tile")),
        P(("track", "tile")),
        P(("track", "tile"), None),
        P(("track", "tile"), None),
        P(("track", "tile")),
    )
    out_specs = (P(("track", "tile"), None, None), P(("track", "tile")))
    return jax.shard_map(
        on_device, mesh=mesh, in_specs=in_specs, out_specs=out_specs, check_vma=False
    )
```

```python
import functools

import jax
import jax.numpy as jnp
from jax import lax
from jax.experimental import pallas as pl
from jax.experimental.pallas import tpu as pltpu
from jax.sharding import PartitionSpec as P

F32 = jnp.float32
BF16 = jnp.bfloat16
MESH = pl.DeviceIdType.MESH
CHUNK = 256
NT = (((1,), (1,)), ((), ()))


def sincos(x):
    q = jnp.floor(x * 0.6366197723675814 + 0.5)
    r = ((x - q * 1.5703125) - q * 4.837512969970703e-4) - q * 7.549789948768648e-8
    r2 = r * r
    s = r + r * r2 * (-1.6666654611e-1 + r2 * (8.3321608736e-3 + r2 * -1.9515295891e-4))
    c = 1.0 - 0.5 * r2 + r2 * r2 * (
        4.166664568298827e-2 + r2 * (-1.388731625493765e-3 + r2 * 2.443315711809948e-5)
    )
    n = q.astype(jnp.int32)
    odd = (n & 1) == 1
    sine = jnp.where(odd, c, s)
    cosine = jnp.where(odd, s, c)
    sine = jnp.where((n & 2) == 2, -sine, sine)
    cosine = jnp.where(((n + 1) & 2) == 2, -cosine, cosine)
    return sine, cosine


def pack(block):
    half = block.shape[2] // 2
    return jnp.concatenate([block[:, :, :half], block[:, :, half:]], axis=1).astype(BF16)


def unpack(block):
    wide = block.astype(F32)
    rows = wide.shape[1] // 2
    return jnp.concatenate([wide[:, :rows], wide[:, rows:]], axis=2)


def kernel(
    n_track, n_tile, tiles_here, ping_local, slots,
    classes_hbm, counts_hbm, panels_hbm, phases_hbm, weights_hbm, send_hbm, foot_hbm,
    image, gradient,
    classes_in, counts_in, panels, phases, weights, send, foot,
    column, gath, e_r, e_i, step_r, step_i, z, om, q_coef, q_sum, marks, mark_out, m_near, m_out, m_in,
    part, near_out, near_in, tile_out, tile_in, h_all,
    l_s, n_ss, n_rs, m_ss, m_rs, b_ss, b_rs, c_ss, c_rs, d_ss, d_rs, e_ss, e_rs,
):
    a = lax.axis_index("track")
    b = lax.axis_index("tile")
    rows_total, width = panels.shape
    bins = width // 2
    classes, pixels, _ = weights.shape
    chunks = pixels // CHUNK
    half = CHUNK // 2
    cap = slots // n_tile
    group_rows = 2 * tiles_here
    tile_rows = n_tile * group_rows
    mark_rows = m_out.shape[0]
    rows_per_ping = rows_total // ping_local
    device = a * n_tile + b
    ping_total = n_track * n_tile * ping_local
    tile_total = n_track * n_tile * tiles_here
    ping_step = n_track / ping_total
    tile_step = n_track / tile_total
    centre = 0.5 * n_track
    inside = {0: a >= 1, 2: a <= n_track - 2}

    def guarded(o, body):
        def run():
            body()
        if o == 1:
            run()
        else:
            pl.when(inside[o])(run)

    def peer(track, tile):
        return {"track": track, "tile": tile}

    def each_peer(o, act):
        for d in range(1 if o == 1 else 0, n_tile):
            act(lax.rem(b + d, n_tile))

    loads = [
        pltpu.make_async_copy(source, target, l_s.at[n])
        for n, (source, target) in enumerate((
            (foot_hbm, foot), (counts_hbm, counts_in), (classes_hbm, classes_in), (send_hbm, send),
            (phases_hbm, phases), (panels_hbm, panels), (weights_hbm, weights),
        ))
    ]
    for load in loads:
        load.start()

    barrier = pltpu.get_barrier_semaphore()
    for o in range(3):
        guarded(o, lambda o=o: each_peer(o, lambda s: pl.semaphore_signal(
            barrier, inc=1, device_id=peer(a + o - 1, s), device_id_type=MESH)))

    for load in loads[:5]:
        load.wait()
    entry = lax.broadcasted_iota(jnp.int32, (1, foot.shape[1]), 1)
    used = []
    for t in range(tiles_here):
        used.append(jnp.where(entry < counts_in[t], foot[t:t + 1, :], -1))
    used = jnp.concatenate(used + used, axis=0).astype(F32)
    used = used.T
    slot_lane = lax.broadcasted_iota(jnp.int32, (foot.shape[1], 3 * slots), 1).astype(F32)
    for t in range(tiles_here):
        hit = jnp.where(used[:, t:t + 1] == slot_lane, 1.0, 0.0)
        hit = jnp.max(hit, axis=0, keepdims=True) * (classes_in[t] + 1).astype(F32)
        for k in range(3):
            mark_out[k, t:t + 1, :] = hit[:, k * slots:(k + 1) * slots]
            mark_out[k, tiles_here + t:tiles_here + t + 1, :] = hit[:, k * slots:(k + 1) * slots]

    neighbours = (
        n_tile - 1
        + n_tile * (jnp.where(a >= 1, 1, 0) + jnp.where(a <= n_track - 2, 1, 0))
    )
    pl.semaphore_wait(barrier, neighbours)

    def mark_step(k):
        return pltpu.make_async_remote_copy(
            src_ref=mark_out.at[k], dst_ref=m_near.at[2 - k],
            send_sem=n_ss.at[k], recv_sem=n_rs.at[2 - k],
            device_id=peer(a + k - 1, b), device_id_type=MESH,
        )

    def mark_copy(s, slot):
        return pltpu.make_async_remote_copy(
            src_ref=m_out, dst_ref=m_in.at[slot],
            send_sem=m_ss.at[s], recv_sem=m_rs.at[slot],
            device_id=peer(a, s), device_id_type=MESH,
        )

    for k in (0, 2):
        guarded(k, lambda k=k: mark_step(k).start())
    m_near[1] = mark_out[1]
    blank = jnp.zeros((n_tile, 2 * group_rows, half), BF16)
    for c in range(chunks):
        tile_in[c, b] = blank[0]
    for o in (0, 2):
        @pl.when(jnp.logical_not(inside[o]))
        def _(o=o):
            m_near[o] = jnp.zeros((group_rows, slots), F32)
            for c in range(chunks):
                h_all[c, o] = blank

    def ping_places(rows):
        ping = device * ping_local + rows // rows_per_ping
        return (ping.astype(F32) + 0.5) * ping_step - centre

    line = jnp.concatenate([send[n:n + 1, :] for n in range(send.shape[0])], axis=1)
    owner = line // rows_per_ping
    phase = jnp.broadcast_to(phases[...], (8, ping_local)).T[:, :1]
    ping = lax.broadcasted_iota(jnp.int32, (ping_local, 3 * slots), 0)
    angle = jnp.sum(jnp.where(ping == owner, phase, 0.0), axis=0, keepdims=True)
    sine, cosine = sincos(angle)
    place = ping_places(line)
    half_i, half_r = sincos((96.0 * half / pixels) * place)
    full_i, full_r = sincos((96.0 * CHUNK / pixels) * place)
    lines = jnp.concatenate(
        [line.astype(F32), cosine, sine, place, half_r, half_i, full_r, full_i], axis=0
    )
    column[...] = lines.T

    def grids(o, carry):
        mine = column[pl.ds(pl.multiple_of(o * slots, slots), slots), :]
        place = mine[:, 3:4]
        lane = lax.broadcasted_iota(jnp.int32, (slots, half), 1).astype(F32)
        across = (lane + 0.5) * (1.0 / pixels) - 0.5
        first_i, first_r = sincos(96.0 * across * place + 8.0 * (place * place))
        half_r, half_i = mine[:, 4:5], mine[:, 5:6]
        e_r[o, :, :half] = first_r
        e_i[o, :, :half] = first_i
        e_r[o, :, half:] = first_r * half_r - first_i * half_i
        e_i[o, :, half:] = first_r * half_i + first_i * half_r
        step_r[o] = jnp.broadcast_to(mine[:, 6:7], (slots, CHUNK))
        step_i[o] = jnp.broadcast_to(mine[:, 7:8], (slots, CHUNK))
        return carry

    lax.fori_loop(0, 3, grids, 0)
    for o in (0, 2):
        guarded(o, lambda o=o: mark_step(2 - o).wait_recv())
    near = [m_near[o, :tiles_here] for o in range(3)]
    near = jnp.concatenate(near + [jnp.zeros((mark_rows - 3 * tiles_here, slots), F32)], axis=0)
    m_out[...] = near.astype(BF16)
    m_in[b] = near.astype(BF16)
    each_peer(1, lambda s: mark_copy(s, b).start())

    loads[5].wait()
    local = column[:, 0:1].astype(jnp.int32)
    chosen = lax.broadcasted_iota(jnp.int32, (3 * slots, rows_total), 1) == local
    chosen = jnp.where(chosen, 1.0, 0.0).astype(BF16)
    for start in range(0, bins, CHUNK):
        real = jnp.dot(chosen, panels[:, start:start + CHUNK], preferred_element_type=F32)
        imag = jnp.dot(
            chosen, panels[:, bins + start:bins + start + CHUNK], preferred_element_type=F32
        )
        for o in range(3):
            rows = slice(o * slots, (o + 1) * slots)
            cosine = jnp.broadcast_to(column[rows, 1:2], (slots, CHUNK))
            sine = jnp.broadcast_to(column[rows, 2:3], (slots, CHUNK))
            gath[o, :slots, start:start + CHUNK] = (cosine * real[rows] - sine * imag[rows]).astype(BF16)
            gath[o, slots:, start:start + CHUNK] = (sine * real[rows] + cosine * imag[rows]).astype(BF16)

    each_peer(1, lambda s: mark_copy(s, s).wait_recv())
    lane = lax.broadcasted_iota(jnp.int32, (mark_rows, slots), 1)
    got_marks = []
    for s in range(n_tile):
        shifted = pltpu.roll(m_in[s].astype(F32), lax.rem(s - b + n_tile, n_tile) * cap, 1)
        got_marks.append(jnp.where((lane >= s * cap) & (lane < (s + 1) * cap), shifted, 0.0))
    for o in range(3):
        mark = []
        for s in range(n_tile):
            rows = got_marks[s][o * tiles_here:(o + 1) * tiles_here]
            mark += [rows, rows]
        mark = jnp.concatenate(mark, axis=0)
        row = lax.broadcasted_iota(jnp.int32, (tile_rows, slots), 0)
        group = row // group_rows
        real_row = (row - group * group_rows) < tiles_here
        tile = ((a + o - 1) * n_tile + group) * tiles_here + lax.rem(row, tiles_here)
        at = (tile.astype(F32) + 0.5) * tile_step - centre
        w_i, w_r = sincos(-16.0 * at * place[:, o * slots:(o + 1) * slots])
        marks[o, :, :slots] = mark
        marks[o, :, slots:] = mark
        q_coef[o, :, :slots] = jnp.where(real_row, -w_i, w_r)
        q_coef[o, :, slots:] = jnp.where(real_row, -w_r, -w_i)
        coef = jnp.concatenate(
            [jnp.where(real_row, w_r, w_i), jnp.where(real_row, -w_i, w_r)], axis=1
        )
        mark = jnp.concatenate([mark, mark], axis=1)
        for k in range(classes):
            value = jnp.where(mark == k + 1.0, coef, 0.0)
            high = value.astype(BF16)
            om[o, k, :tile_rows] = high
            om[o, k, tile_rows:] = (value - high.astype(F32)).astype(BF16)
    q_sum[...] = jnp.zeros_like(q_sum)
    loads[6].wait()

    def near_copy(c, j):
        return pltpu.make_async_remote_copy(
            src_ref=near_out.at[c, j], dst_ref=near_in.at[c, j],
            send_sem=b_ss.at[c, j], recv_sem=b_rs.at[c, j],
            device_id=peer(a + 2 * j - 1, b), device_id_type=MESH,
        )

    def tile_copy(c, s, slot):
        return pltpu.make_async_remote_copy(
            src_ref=tile_out.at[c, s], dst_ref=tile_in.at[c, slot],
            send_sem=c_ss.at[c, s], recv_sem=c_rs.at[c, slot],
            device_id=peer(a, s), device_id_type=MESH,
        )

    def h_copy(c, s, slot):
        return pltpu.make_async_remote_copy(
            src_ref=h_all.at[c, 1, b], dst_ref=h_all.at[c, 1, slot],
            send_sem=d_ss.at[c, s], recv_sem=d_rs.at[c, slot],
            device_id=peer(a, s), device_id_type=MESH,
        )

    def h_forward(c, o):
        return pltpu.make_async_remote_copy(
            src_ref=h_all.at[c, 1], dst_ref=h_all.at[c, 2 - o],
            send_sem=e_ss.at[c, o // 2], recv_sem=e_rs.at[c, o // 2],
            device_id=peer(a + o - 1, b), device_id_type=MESH,
        )

    def project(c):
        totals = [None, None, None]
        for k in range(classes):
            weight = weights[k, pl.ds(pl.multiple_of(c * CHUNK, CHUNK), CHUNK), :]
            every = lax.dot_general(
                gath[...].reshape(6 * slots, bins), weight, NT, preferred_element_type=F32
            )
            for o in (0, 2, 1):
                y = every[2 * o * slots:2 * (o + 1) * slots]
                turn_r, turn_i = e_r[o], e_i[o]
                turned = jnp.concatenate(
                    [turn_r * y[:slots] - turn_i * y[slots:], turn_i * y[:slots] + turn_r * y[slots:]],
                    axis=0,
                ).astype(BF16)
                z[c, o, k] = turned
                got = jnp.dot(om[o, k], turned, preferred_element_type=F32)
                totals[o] = got if k == 0 else totals[o] + got
        for o in range(3):
            total = (totals[o][:tile_rows] + totals[o][tile_rows:]).reshape(n_tile, group_rows, CHUNK)
            if o == 1:
                part[c] = total
            else:
                near_out[c, o // 2] = pack(total)
        for o in (0, 2):
            guarded(o, lambda o=o: near_copy(c, o // 2).start())
        for o in range(3):
            now_r, now_i, by_r, by_i = e_r[o], e_i[o], step_r[o], step_i[o]
            e_r[o] = now_r * by_r - now_i * by_i
            e_i[o] = now_r * by_i + now_i * by_r

    def reduce_tracks(c):
        for j in range(2):
            def add(j=j):
                near_copy(c, j).wait_recv()
                part[c] += unpack(near_in[c, j])
            guarded(2 - 2 * j, add)
        tile_out[c] = pack(part[c])
        each_peer(1, lambda s: tile_copy(c, s, b).start())

    def reduce_tiles(c):
        each_peer(1, lambda s: tile_copy(c, s, s).wait_recv())
        arrived = unpack(tile_in[c])
        own = part[c, b]
        for s in range(n_tile):
            own = own + arrived[s]
        s_r, s_i = own[:tiles_here], own[tiles_here:]
        power = s_r * s_r + s_i * s_i
        heavy = jnp.concatenate([power * s_r, power * s_i], axis=0)
        h_all[c, 1, b] = pack(heavy[None])[0]
        each_peer(1, lambda s: h_copy(c, s, b).start())
        tile_ids = device * tiles_here + lax.broadcasted_iota(jnp.int32, (tiles_here, CHUNK), 0)
        at = (tile_ids.astype(F32) + 0.5) * tile_step - centre
        pixel = c * CHUNK + lax.broadcasted_iota(jnp.int32, (tiles_here, CHUNK), 1)
        across = (pixel.astype(F32) + 0.5) * (1.0 / pixels) - 0.5
        t_i, t_r = sincos(8.0 * (at * at) - 96.0 * across * at)
        out_r = t_r * s_r - t_i * s_i
        out_i = t_i * s_r + t_r * s_i
        here = pl.ds(pl.multiple_of(c * CHUNK, CHUNK), CHUNK)
        for t in range(tiles_here):
            image[t, 0:1, here] = out_r[t:t + 1]
            image[t, 1:2, here] = out_i[t:t + 1]

    def relay(c):
        each_peer(1, lambda s: h_copy(c, s, s).wait_recv())
        for o in (0, 2):
            guarded(o, lambda o=o: h_forward(c, o).start())

    def pull(c):
        for o in (1, 0, 2):
            if o != 1:
                guarded(o, lambda o=o: h_forward(c, 2 - o).wait_recv())
            heavy = unpack(h_all[c, o]).reshape(tile_rows, CHUNK).astype(BF16)
            mark = marks[o]
            total = jnp.zeros((tile_rows, 2 * slots), F32)
            for k in range(classes):
                got = lax.dot_general(heavy, z[c, o, k], NT, preferred_element_type=F32)
                total = jnp.where(mark == k + 1.0, got, total)
            q_sum[o] += total

    def stage(i, carry):
        for lag, act in enumerate((project, reduce_tracks, reduce_tiles, relay, pull)):
            @pl.when((i >= lag) & (i < chunks + lag))
            def _(lag=lag, act=act):
                act(i - lag)
        return carry

    lax.fori_loop(0, chunks + 4, stage, 0)

    ping = lax.broadcasted_iota(jnp.int32, (ping_local, slots), 0)
    spread = jnp.zeros((ping_local, slots), F32)
    for o in range(3):
        corr = jnp.sum(q_sum[o] * q_coef[o], axis=0, keepdims=True)
        corr = corr[:, :slots] + corr[:, slots:]
        mine = line[:, o * slots:(o + 1) * slots]
        spread = spread + jnp.where(mine // rows_per_ping == ping, corr, 0.0)
    sums = jnp.sum(spread, axis=1, keepdims=True)
    gradient[...] = jnp.broadcast_to(sums, (ping_local, 128)).T[:1]

    for k in (0, 2):
        guarded(k, lambda k=k: mark_step(k).wait_send())
    each_peer(1, lambda s: mark_copy(s, b).wait_send())

    def finish(c, carry):
        for o in (0, 2):
            def sent(o=o):
                near_copy(c, o // 2).wait_send()
                h_forward(c, o).wait_send()
            guarded(o, sent)
        each_peer(1, lambda s: tile_copy(c, s, b).wait_send())
        each_peer(1, lambda s: h_copy(c, s, b).wait_send())
        return carry

    lax.fori_loop(0, chunks, finish, 0)


def on_device(
    panels, phases, weight_tiles, tile_class, send_slots, foot_slot, foot_ping, tile_counts
):
    n_track = lax.axis_size("track")
    n_tile = lax.axis_size("tile")
    ping_local = phases.shape[0]
    rows_total, width = panels.shape
    bins = width // 2
    tiles_here, foot = foot_slot.shape
    classes, pixels, _ = weight_tiles.shape
    slots = send_slots.shape[0] // 3
    group_rows = 2 * tiles_here
    tile_rows = n_tile * group_rows
    chunks = pixels // CHUNK
    mark_rows = -(-3 * tiles_here // 16) * 16
    packed = (n_tile, 2 * group_rows, CHUNK // 2)
    vmem = pl.BlockSpec(memory_space=pltpu.VMEM)
    hbm = pl.BlockSpec(memory_space=pltpu.HBM)
    dma = pltpu.SemaphoreType.DMA
    image, gradient = pl.pallas_call(
        functools.partial(kernel, n_track, n_tile, tiles_here, ping_local, slots),
        out_shape=(
            jax.ShapeDtypeStruct((tiles_here, 2, pixels), F32),
            jax.ShapeDtypeStruct((1, ping_local), F32),
        ),
        in_specs=[hbm] * 7,
        out_specs=(vmem, vmem),
        scratch_shapes=[
            pltpu.SMEM((tiles_here,), jnp.int32),
            pltpu.SMEM((tiles_here,), jnp.int32),
            pltpu.VMEM((rows_total, width), BF16),
            pltpu.VMEM((1, ping_local), F32),
            pltpu.VMEM((classes, pixels, bins), BF16),
            pltpu.VMEM((3 * slots // 128, 128), jnp.int32),
            pltpu.VMEM((tiles_here, foot), jnp.int32),
            pltpu.VMEM((3 * slots, 8), F32),
            pltpu.VMEM((3, 2 * slots, bins), BF16),
            pltpu.VMEM((3, slots, CHUNK), F32),
            pltpu.VMEM((3, slots, CHUNK), F32),
            pltpu.VMEM((3, slots, CHUNK), F32),
            pltpu.VMEM((3, slots, CHUNK), F32),
            pltpu.VMEM((chunks, 3, classes, 2 * slots, CHUNK), BF16),
            pltpu.VMEM((3, classes, 2 * tile_rows, 2 * slots), BF16),
            pltpu.VMEM((3, tile_rows, 2 * slots), F32),
            pltpu.VMEM((3, tile_rows, 2 * slots), F32),
            pltpu.VMEM((3, tile_rows, 2 * slots), F32),
            pltpu.VMEM((3, group_rows, slots), F32),
            pltpu.VMEM((3, group_rows, slots), F32),
            pltpu.VMEM((mark_rows, slots), BF16),
            pltpu.VMEM((n_tile, mark_rows, slots), BF16),
            pltpu.VMEM((chunks, n_tile, group_rows, CHUNK), F32),
            pltpu.VMEM((chunks, 2) + packed, BF16),
            pltpu.VMEM((chunks, 2) + packed, BF16),
            pltpu.VMEM((chunks,) + packed, BF16),
            pltpu.VMEM((chunks,) + packed, BF16),
            pltpu.VMEM((chunks, 3) + packed, BF16),
            dma((7,)),
            dma((3,)), dma((3,)),
            dma((n_tile,)), dma((n_tile,)),
            dma((chunks, 2)), dma((chunks, 2)),
            dma((chunks, n_tile)), dma((chunks, n_tile)),
            dma((chunks, n_tile)), dma((chunks, n_tile)),
            dma((chunks, 2)), dma((chunks, 2)),
        ],
        compiler_params=pltpu.CompilerParams(
            collective_id=0, has_side_effects=True, vmem_limit_bytes=56 * 1024 * 1024
        ),
    )(
        tile_class, tile_counts, panels, phases.reshape(1, ping_local), weight_tiles,
        send_slots.reshape(3 * slots // 128, 128), foot_slot,
    )
    return image, gradient.reshape(ping_local)


def solution(mesh):
    in_specs = (
        P(("track", "tile"), None),
        P(("track", "tile")),
        P(),
        P(("track", "tile")),
        P(("track", "tile")),
        P(("track", "tile"), None),
        P(("track", "tile"), None),
        P(("track", "tile")),
    )
    out_specs = (P(("track", "tile"), None, None), P(("track", "tile")))
    return jax.shard_map(
        on_device, mesh=mesh, in_specs=in_specs, out_specs=out_specs, check_vma=False
    )
```
